1024 devices in a mesh: seq: 64 (over y, z_hi, core), dp: 16 (over z_lo, x).
Axes of the slice: x: 8, y: 8, z: 8 (z_hi: 4, z_lo: 2; z = z_hi * 2 + z_lo), core: 2. Of those that a mesh axis runs over, the one named last changes fastest.
Arguments:
- projected: bfloat16 [3, 32768, 4096], P(None, 'seq', 'dp'), may hold values from -6 to 6
- featurizer: bfloat16 [7, 3, 4096], P(None, None, 'dp'), may hold values from -25 to 25
- long_filter: bfloat16 [256, 128], P('dp'), may hold values from -0.5 to 0.5
- skip_gain: bfloat16 [4096], P('dp'), may hold values from -4 to 4
- out_cotangent: bfloat16 [32768, 4096], P('seq', 'dp'), may hold values from -6 to 6
Outputs:
- grad_featurizer: float32 [7, 3, 4096], P(None, None, 'dp')
- grad_filter: float32 [256, 128], P('dp')
- grad_skip: float32 [4096], P('dp')
The draws below stay inside these ranges and needn't reach their ends.
All inputs are finite; a program needn't handle non-finite values.
Results may differ from the reference program's by a relative error of at most 0.0071.
Values may be sent and summed in bfloat16 or wider, within the bound.
A program may use at most 32 MiB of HBM per device.

```python
import math
import jax
import jax.numpy as jnp
from jax import lax

D = 4096
GS = 16
L = 128
FEAT = 7
G = 256
TOKENS = 32768


def draw_featurizer(key, part):
    noise_key = jax.random.fold_in(key, 11)
    position = jnp.arange(D, dtype=jnp.float32) / (D - 1)
    base = jnp.clip(jax.random.normal(noise_key, (FEAT, 3, D), jnp.float32), -4.0, 4.0)
    rising = 10.0 ** position
    scales = jnp.stack([rising, jnp.ones_like(rising), jnp.ones_like(rising)])
    return (base * scales[None] / math.sqrt(FEAT)).astype(jnp.bfloat16)


def levels(stream_key, dims, pieces, smallest, high):
    def one(dim, blocks):
        draws = jax.random.uniform(jax.random.fold_in(jax.random.fold_in(stream_key, 6), dim), (blocks,), jnp.float32, smallest / len(pieces), high / len(pieces))
        return jnp.repeat(jnp.exp(draws), dims[dim] // blocks).reshape((-1,) + (1,) * (len(dims) - dim - 1))

    gain = one(*pieces[0])
    for cut in pieces[1:]:
        gain = gain * one(*cut)
    return gain


def bell_draw(key, shape, width, limit, pieces=(), kind=jnp.bfloat16):
    entries = jax.random.normal(key, shape, jnp.float32) * width
    if len(pieces) > 0:
        entries = levels(key, shape, pieces, -0.22, 0.18) * entries
    return jnp.clip(entries, min=-limit, max=limit).astype(kind)


def setup_inputs(seed: int = 0) -> dict:
    streams_of = jax.random.split(jax.random.key(seed), 6)
    return {
        "projected": bell_draw(streams_of[0], (3, TOKENS, D), 1.0, 6.0, ((1, 64), (2, 16))),
        "featurizer": draw_featurizer(jax.random.fold_in(streams_of[5], 71), 0),
        "long_filter": bell_draw(streams_of[2], (G, L), L ** -0.5, 0.5, ((0, 16),)),
        "skip_gain": bell_draw(streams_of[3], (D,), 1.0, 4.0, ((0, 16),)),
        "out_cotangent": bell_draw(streams_of[4], (TOKENS, D), 1.0, 6.0, ((0, 64), (1, 16))),
    }


def settle(values):
    return lax.optimization_barrier(values.astype(jnp.bfloat16)).astype(jnp.float32)

def causal(signal, kernel, fft_size, keep_rows):
    spectrum = jnp.fft.rfft(signal, n=fft_size, axis=0) * jnp.fft.rfft(kernel, n=fft_size, axis=0)
    return jnp.fft.irfft(spectrum, n=fft_size, axis=0)[:keep_rows]

def reference(projected, featurizer, long_filter, skip_gain, out_cotangent):
    token_scale = 1.0 / math.sqrt(TOKENS)
    fft_size = 2 ** (TOKENS + L - 1).bit_length()
    width_block = math.gcd(D, 256)
    group_block = width_block // GS
    block_count = D // width_block
    starts = jnp.arange(block_count, dtype=jnp.int32) * width_block

    def forward(start):
        source = lax.dynamic_slice_in_dim(projected, start, width_block, 2).astype(jnp.float32)
        taps = lax.dynamic_slice_in_dim(featurizer, start, width_block, 2).astype(jnp.float32)
        filters = lax.dynamic_slice_in_dim(long_filter, start // GS, group_block, 0).astype(jnp.float32)
        skip = lax.dynamic_slice_in_dim(skip_gain, start, width_block, 0).astype(jnp.float32)
        padded = jnp.pad(source, ((0, 0), (FEAT - 1, 0), (0, 0)))
        featured = jnp.zeros_like(source)
        for tap_index in range(FEAT):
            begin = FEAT - 1 - tap_index
            featured = featured + taps[tap_index][:, None, :] * padded[:, begin:begin + TOKENS]
        rounded = settle(featured)
        queries = rounded[0]
        key_part = rounded[1]
        value_part = rounded[2]
        product = settle(key_part * value_part)
        kernel = jnp.repeat(filters.T, GS, axis=1)
        filtered = causal(product, kernel, fft_size, TOKENS)
        inner_sum = filtered + skip * product
        output = queries * inner_sum
        return (padded, queries, key_part, value_part, product, kernel, skip, inner_sum, output)

    def stats(carry, start):
        output = forward(start)[8]
        cot = lax.dynamic_slice_in_dim(out_cotangent, start, width_block, 1).astype(jnp.float32)
        return ((carry[0] + lax.optimization_barrier(jnp.sum(output * output, axis=1)), carry[1] + lax.optimization_barrier(jnp.sum(cot * output, axis=1))), None)
    initial = (jnp.zeros((TOKENS,), jnp.float32), jnp.zeros((TOKENS,), jnp.float32))
    sums, unused = lax.scan(stats, initial, starts)
    rms = jnp.sqrt(sums[0] / D + 1e-05)
    cross_mean = sums[1] / D

    def grads(start):
        padded, queries, key_part, value_part, product, kernel, skip, inner_sum, output = forward(start)
        cot = lax.dynamic_slice_in_dim(out_cotangent, start, width_block, 1).astype(jnp.float32)
        out_grad = (cot / rms[:, None] - output * (cross_mean / rms ** 3)[:, None]) * token_scale
        conv_grad = out_grad * queries
        cotangent = settle(conv_grad)
        query_grad = out_grad * inner_sum
        backward = jnp.flip(causal(jnp.flip(cotangent, 0), kernel, fft_size, TOKENS), 0)
        product_grad = backward + skip * conv_grad
        all_grad = jnp.stack([query_grad, product_grad * value_part, product_grad * key_part])
        feat_grad = jnp.stack([lax.optimization_barrier(jnp.sum(all_grad * padded[:, FEAT - 1 - tap_index:FEAT - 1 - tap_index + TOKENS], axis=1)) for tap_index in range(FEAT)])
        skip_grad = lax.optimization_barrier(jnp.sum(conv_grad * product, axis=0))
        spectra = jnp.fft.rfft(cotangent, n=fft_size, axis=0) * jnp.conj(jnp.fft.rfft(product, n=fft_size, axis=0))
        lagged = jnp.fft.irfft(spectra, n=fft_size, axis=0)[:L]
        filter_grad = lagged.reshape(L, group_block, GS).sum(axis=2).T
        return (feat_grad, filter_grad, skip_grad)
    feat_all, filter_all, skip_all = lax.map(grads, starts)
    grad_featurizer = jnp.moveaxis(feat_all, 0, 2).reshape(FEAT, 3, D)
    grad_filter = filter_all.reshape(G, L)
    grad_skip = skip_all.reshape(D)
    return (grad_featurizer, grad_filter, grad_skip)
```

```python
import functools
import math

import jax
import jax.numpy as jnp
from jax import lax
from jax.experimental import pallas as pl
from jax.experimental.pallas import tpu as pltpu
from jax.sharding import PartitionSpec as P

F32 = jnp.float32
BF16 = jnp.bfloat16
LANES = 128
MEMBERS = 16
HALO = 144
MESH = pl.DeviceIdType.MESH


def iota(shape, dim):
    return lax.broadcasted_iota(jnp.int32, shape, dim)


def dot(lhs, rhs):
    return lax.dot_general(lhs, rhs, (((1,), (0,)), ((), ())), preferred_element_type=F32)


def dot_nt(lhs, rhs):
    return lax.dot_general(lhs, rhs, (((1,), (1,)), ((), ())), preferred_element_type=F32)


def aligned(index, step):
    return pl.multiple_of(index * step, step)


def fold(array):
    total = array[0:8]
    for begin in range(8, array.shape[0], 8):
        total = total + array[begin : begin + 8]
    return total


def kernel(geo, proj, taps, filt, skip, cot, out_f, out_l, out_s,
           pb, cb, tr, lf, sk, lff, wv, pf, kv, qv, xt, qt, gt, innt, ut, wt, inn, tof, tob, xg,
           pgt, skt, at, bt, st, acc, sla, slb, slc,
           ld_sem, h_s, h_r, s_s, s_r, a_s, a_r, b_s, b_r, c_s, c_r):
    n_seq, n_dp, n_y, n_z, rows, n_taps, channels = geo
    blocks = rows // LANES
    groups = channels // MEMBERS
    cts = channels // LANES
    me = lax.axis_index("seq")
    md = lax.axis_index("dp")
    my = me // n_z
    mz = lax.rem(me, n_z)
    mine = 64 // n_y

    loads = [
        pltpu.make_async_copy(filt, lf, ld_sem.at[0]),
        pltpu.make_async_copy(taps, tr, ld_sem.at[1]),
        pltpu.make_async_copy(skip, sk, ld_sem.at[2]),
        pltpu.make_async_copy(proj, pb.at[:, pl.ds(HALO, rows), :], ld_sem.at[3]),
        pltpu.make_async_copy(cot, cb, ld_sem.at[4]),
    ]
    for copy in loads:
        copy.start()

    barrier = pltpu.get_barrier_semaphore()

    def dp_peer(i):
        return {"dp": lax.rem(md + i, n_dp)}

    def y_index(i):
        return lax.rem(my + i, n_y)

    def y_peer(i):
        return {"seq": y_index(i) * n_z + mz}

    def z_peer(i):
        return {"seq": my * n_z + lax.rem(mz + i, n_z)}

    def greet(peer, count):
        @pl.loop(1, count)
        def _(i):
            pl.semaphore_signal(barrier, 1, device_id=peer(i), device_id_type=MESH)

    ahead = {"seq": lax.rem(me + 1, n_seq)}
    behind = {"seq": lax.rem(me + n_seq - 1, n_seq)}
    pl.semaphore_signal(barrier, 1, device_id=behind, device_id_type=MESH)
    pl.semaphore_signal(barrier, 1, device_id=ahead, device_id_type=MESH)
    greet(dp_peer, n_dp)
    greet(y_peer, n_y)
    greet(z_peer, n_z)

    for copy in loads[:3]:
        copy.wait()
    lff[...] = lf[...].astype(F32)
    for p in range(3):
        wv[p, 0:n_taps, :] = tr[p].astype(F32)
    row8 = iota((8, LANES), 0)
    keep = iota((LANES, LANES), 1) >= iota((LANES, LANES), 0)

    @pl.loop(0, groups)
    def _(g):
        base = jnp.broadcast_to(lff[pl.ds(g, 1), :], (8, LANES))
        for k in (1, 2, 4):
            base = jnp.where((row8 & k) != 0, pltpu.roll(base, k, 1), base)
        tiles = [base] + [pltpu.roll(base, 8 * r, 1) for r in range(1, LANES // 8)]
        circ = jnp.concatenate(tiles, axis=0)
        near = jnp.where(keep, circ, 0.0).astype(BF16)
        far = jnp.where(keep, 0.0, circ).astype(BF16)
        tof[g, 0:LANES, :] = far
        tof[g, LANES : 2 * LANES, :] = near
        tob[g, :, 0:LANES] = near
        tob[g, :, LANES : 2 * LANES] = far

    for ct in range(cts):
        cols = slice(ct * LANES, (ct + 1) * LANES)
        line = jnp.broadcast_to(sk[:, cols].astype(F32), (LANES, LANES))
        skt[cols, :] = line.T

    pl.semaphore_wait(barrier, n_dp + n_y + n_z - 1)
    halo = [
        pltpu.make_async_remote_copy(
            src_ref=proj.at[pl.ds(1, 2), pl.ds(rows - HALO, HALO), :],
            dst_ref=pb.at[pl.ds(1, 2), pl.ds(0, HALO), :],
            send_sem=h_s.at[0], recv_sem=h_r.at[0], device_id=ahead, device_id_type=MESH),
        pltpu.make_async_remote_copy(
            src_ref=proj.at[pl.ds(0, 1), pl.ds(rows - 16, 16), :],
            dst_ref=pb.at[pl.ds(0, 1), pl.ds(HALO - 16, 16), :],
            send_sem=h_s.at[1], recv_sem=h_r.at[1], device_id=ahead, device_id_type=MESH),
    ]

    @pl.when(me < n_seq - 1)
    def _():
        for copy in halo:
            copy.start()

    def featured(p, ct, block):
        window = pf.at[p * cts + ct, pl.ds(aligned(block, LANES), LANES + 16), :]
        total = None
        for j in range(n_taps):
            term = wv[p, j : j + 1, ct * LANES : (ct + 1) * LANES] * window[16 - j : 16 - j + LANES, :]
            total = term if total is None else total + term
        return total.astype(BF16).astype(F32)

    def widen(begin, count):
        for p in range(3):
            for ct in range(cts):
                pf[p * cts + ct, pl.ds(begin, count), :] = pb[
                    p, pl.ds(begin, count), ct * LANES : (ct + 1) * LANES].astype(F32)

    def product_block(block, with_query):
        for ct in range(cts):
            cols = slice(ct * LANES, (ct + 1) * LANES)
            here = pl.ds(aligned(block, LANES), LANES)
            keys = featured(1, ct, block)
            values = featured(2, ct, block)
            kv[ct, here, :] = keys
            kv[cts + ct, here, :] = values
            product = (keys * values).astype(BF16)
            xt[cols, here] = product.astype(F32).T.astype(BF16)
            if with_query:
                inside = pl.ds(aligned(block - 1, LANES), LANES)
                queries = featured(0, ct, block)
                qv[ct, inside, :] = queries
                qt[cols, inside] = queries.T
                gt[cols, inside] = cb[inside, cols].astype(F32).T

    loads[3].wait()

    @pl.loop(0, blocks)
    def _(block):
        widen(pl.multiple_of(HALO + block * LANES, 16), LANES)

    loads[4].wait()

    @pl.loop(2, blocks + 1)
    def _(block):
        product_block(block, True)

    @pl.when(me > 0)
    def _():
        for copy in halo:
            copy.wait_recv()

    @pl.when(me == 0)
    def _():
        pb[:, 0:HALO, :] = jnp.zeros((3, HALO, channels), BF16)

    widen(0, HALO)
    product_block(0, False)
    product_block(1, True)

    zero8 = jnp.zeros((8, LANES), F32)

    def forward(g, sums):
        sums = list(sums)
        r = pl.ds(aligned(g, MEMBERS), MEMBERS)
        source = [xt[r, b * LANES : (b + 1) * LANES] for b in range(blocks + 1)]
        left = jnp.concatenate(
            [jnp.concatenate([source[b], source[b + 1]], axis=1) for b in range(blocks)], axis=0)
        filtered = dot(left, tof[g])
        gain = skt[r, :]
        for b in range(blocks):
            cols = slice(b * LANES, (b + 1) * LANES)
            inner = filtered[b * MEMBERS : (b + 1) * MEMBERS] + gain * source[b + 1].astype(F32)
            queries = qt[r, cols]
            output = queries * inner
            cotangent = gt[r, cols]
            sums[b] = sums[b] + fold(output * output)
            sums[blocks + b] = sums[blocks + b] + fold(cotangent * output)
            innt[r, cols] = inner
            ut[r, cols] = cotangent * queries
            wt[r, cols] = output * queries
        return tuple(sums)

    sums = lax.fori_loop(0, groups, forward, (zero8,) * (2 * blocks), unroll=4)
    st[md] = jnp.concatenate([jnp.sum(part, axis=0, keepdims=True) for part in sums], axis=0)

    def stat_copy(i):
        return pltpu.make_async_remote_copy(
            src_ref=st.at[md], dst_ref=st.at[md], send_sem=s_s.at[i],
            recv_sem=s_r.at[md], device_id=dp_peer(i), device_id_type=MESH)

    @pl.loop(1, n_dp)
    def _(i):
        stat_copy(i).start()

    @pl.loop(0, blocks)
    def _(block):
        here = pl.ds(aligned(block, LANES), LANES)
        for ct in range(cts):
            inn[ct, here, :] = innt[ct * LANES : (ct + 1) * LANES, here].T

    @pl.loop(0, groups)
    def _(g):
        r = pl.ds(aligned(g, MEMBERS), MEMBERS)
        stack = [xt[r, b * LANES : (b + 1) * LANES].astype(F32) for b in range(blocks + 1)]
        stack.append(jnp.zeros((LANES - (blocks + 1) * MEMBERS, LANES), F32))
        xg[g] = jnp.concatenate(stack, axis=0).T.astype(BF16)

    @pl.loop(1, n_dp)
    def _(i):
        src = lax.rem(md + i, n_dp)
        pltpu.make_async_remote_copy(
            src_ref=st.at[src], dst_ref=st.at[src], send_sem=s_s.at[i],
            recv_sem=s_r.at[src], device_id=dp_peer(i), device_id_type=MESH).wait_recv()

    whole = st[0]
    for i in range(1, n_dp):
        whole = whole + st[i]
    mean = whole * (1.0 / (channels * n_dp))
    token_scale = 1.0 / math.sqrt(rows * n_seq)
    rms = jnp.sqrt(mean[0:blocks] + 1e-05)
    scale_a = token_scale / rms
    scale_b = token_scale * mean[blocks : 2 * blocks] / (rms * rms * rms)
    lines_a = [scale_a[b : b + 1] for b in range(blocks)]
    lines_b = [scale_b[b : b + 1] for b in range(blocks)]
    for b in range(blocks):
        at[b] = jnp.broadcast_to(lines_a[b], (LANES, LANES)).T
        bt[b] = jnp.broadcast_to(lines_b[b], (LANES, LANES)).T

    pad = jnp.zeros((MEMBERS, LANES), BF16)
    fill = jnp.zeros((LANES - (blocks + 1) * MEMBERS, LANES), BF16)

    def backward(g, carry):
        r = pl.ds(aligned(g, MEMBERS), MEMBERS)
        parts = []
        for b in range(blocks):
            cols = slice(b * LANES, (b + 1) * LANES)
            parts.append((ut[r, cols] * lines_a[b] - wt[r, cols] * lines_b[b]).astype(BF16))
        chain = [pad] + parts + [pad]
        left = jnp.concatenate(
            [jnp.concatenate([chain[b], chain[b + 1]], axis=1) for b in range(blocks + 1)], axis=0)
        grad = dot_nt(left, tob[g])
        for b in range(blocks + 1):
            pgt[r, b * LANES : (b + 1) * LANES] = grad[b * MEMBERS : (b + 1) * MEMBERS]
        right = jnp.concatenate(
            [jnp.concatenate(parts + [pad, fill], axis=0), jnp.concatenate([pad] + parts + [fill], axis=0)],
            axis=1)
        lagged = dot(xg[g], right)
        square = jnp.where(keep, lagged[:, LANES:], lagged[:, :LANES])
        total = square[0:8]
        for t in range(1, LANES // 8):
            total = total + pltpu.roll(square[8 * t : 8 * t + 8], LANES - 8 * t, 1)
        for k in (1, 2, 4):
            total = jnp.where((row8 & k) != 0, pltpu.roll(total, LANES - k, 1), total)
        acc[pl.ds(48 + g, 1), :] = jnp.sum(total, axis=0, keepdims=True)
        return carry

    lax.fori_loop(0, groups, backward, 0, unroll=2)

    for ct in range(cts):
        cols = slice(ct * LANES, (ct + 1) * LANES)
        gain = sk[:, cols].astype(F32)

        def taps_of(part, window, begin, count, grad, totals):
            for j in range(n_taps):
                term = grad * window[16 - j + begin : 16 - j + begin + count, :]
                totals[part * 8 + j] = totals[part * 8 + j] + fold(term)

        def tail(block, totals, inside):
            totals = list(totals)
            here = pl.ds(aligned(block, LANES), LANES)
            backed = pgt[cols, here].T
            windows = [
                pf.at[p * cts + ct, pl.ds(aligned(block, LANES), LANES + 16), :] for p in range(3)]
            step = 32
            for begin in range(0, LANES, step):
                local = pl.ds(pl.multiple_of(block * LANES + begin, 8), step)
                keys = kv[ct, local, :]
                values = kv[cts + ct, local, :]
                grad = backed[begin : begin + step]
                if inside:
                    own = pl.ds(pl.multiple_of((block - 1) * LANES + begin, 16), step)
                    queries = qv[ct, own, :]
                    inner = inn[ct, own, :]
                    first = at[block - 1, begin : begin + step, :]
                    second = bt[block - 1, begin : begin + step, :]
                    out_grad = cb[own, cols].astype(F32) * first - queries * inner * second
                    conv = out_grad * queries
                    grad = grad + gain * conv
                    product = (keys * values).astype(BF16).astype(F32)
                    totals[7] = totals[7] + fold(conv * product)
                    taps_of(0, windows[0], begin, step, out_grad * inner, totals)
                taps_of(1, windows[1], begin, step, grad * values, totals)
                taps_of(2, windows[2], begin, step, grad * keys, totals)
            return tuple(totals)

        totals = tail(0, (zero8,) * 24, False)
        totals = lax.fori_loop(1, blocks + 1, functools.partial(tail, inside=True), totals)
        for p in range(3):
            acc[(p * cts + ct) * 8 : (p * cts + ct) * 8 + 8, :] = jnp.concatenate(
                [jnp.sum(totals[p * 8 + j], axis=0, keepdims=True) for j in range(8)], axis=0)

    def a_copy(i):
        there = y_index(i)
        return pltpu.make_async_remote_copy(
            src_ref=acc.at[pl.ds(aligned(there, mine), mine), :], dst_ref=sla.at[my],
            send_sem=a_s.at[i], recv_sem=a_r.at[my], device_id=y_peer(i), device_id_type=MESH)

    def b_copy(i):
        return pltpu.make_async_remote_copy(
            src_ref=slb.at[mz], dst_ref=slb.at[mz],
            send_sem=b_s.at[i], recv_sem=b_r.at[mz], device_id=z_peer(i), device_id_type=MESH)

    def c_copy(i):
        return pltpu.make_async_remote_copy(
            src_ref=slc.at[my], dst_ref=slc.at[my],
            send_sem=c_s.at[i], recv_sem=c_r.at[my], device_id=y_peer(i), device_id_type=MESH)

    def arrived(slots, sends, receives, peer, index, i):
        src = index(i)
        pltpu.make_async_remote_copy(
            src_ref=slots.at[src], dst_ref=slots.at[src], send_sem=sends.at[i],
            recv_sem=receives.at[src], device_id=peer(i), device_id_type=MESH).wait_recv()

    def z_index(i):
        return lax.rem(mz + i, n_z)

    @pl.loop(1, n_y)
    def _(i):
        a_copy(i).start()

    sla[my] = acc[pl.ds(aligned(my, mine), mine), :]

    @pl.loop(1, n_y)
    def _(i):
        arrived(sla, a_s, a_r, y_peer, y_index, i)

    part = sla[0]
    for i in range(1, n_y):
        part = part + sla[i]
    slb[mz] = part

    @pl.loop(1, n_z)
    def _(i):
        b_copy(i).start()

    @pl.loop(1, n_z)
    def _(i):
        arrived(slb, b_s, b_r, z_peer, z_index, i)

    part = slb[0]
    for i in range(1, n_z):
        part = part + slb[i]
    slc[my] = part

    @pl.loop(1, n_y)
    def _(i):
        c_copy(i).start()

    @pl.loop(1, n_y)
    def _(i):
        arrived(slc, c_s, c_r, y_peer, y_index, i)

    def tile(number):
        begin = number * 8
        return slc[begin // mine, begin % mine : begin % mine + 8, :]

    for ct in range(cts):
        cols = slice(ct * LANES, (ct + 1) * LANES)
        for p in range(3):
            out_f[p, :, cols] = tile(p * cts + ct)[0:n_taps]
        out_s[:, cols] = tile(ct)[7:8]
    out_l[0:8, :] = tile(6)
    out_l[8:16, :] = tile(7)

    @pl.loop(1, n_dp)
    def _(i):
        stat_copy(i).wait_send()

    @pl.loop(1, n_y)
    def _(i):
        a_copy(i).wait_send()
        c_copy(i).wait_send()

    @pl.loop(1, n_z)
    def _(i):
        b_copy(i).wait_send()

    @pl.when(me < n_seq - 1)
    def _():
        for copy in halo:
            copy.wait_send()


def body(sizes, projected, featurizer, long_filter, skip_gain, out_cotangent):
    n_seq, n_dp = sizes
    parts, rows, channels = projected.shape
    n_taps = featurizer.shape[0]
    groups, filter_taps = long_filter.shape
    n_y = 1 << ((n_seq.bit_length() - 1) // 2)
    n_z = n_seq // n_y
    blocks = rows // LANES
    cts = channels // LANES
    mine = 64 // n_y
    geo = (n_seq, n_dp, n_y, n_z, rows, n_taps, channels)
    long = rows + LANES
    vmem = pltpu.VMEM
    dma = pltpu.SemaphoreType.DMA
    scratch = [
        vmem((3, HALO + rows, channels), BF16),
        vmem((rows, channels), BF16),
        vmem((3, n_taps, channels), BF16),
        vmem((groups, LANES), BF16),
        vmem((1, channels), BF16),
        vmem((groups, LANES), F32),
        vmem((3, 8, channels), F32),
        vmem((3 * cts, HALO + rows, LANES), F32),
        vmem((2 * cts, long, LANES), F32),
        vmem((cts, rows, LANES), F32),
        vmem((channels, long), BF16),
        vmem((channels, rows), F32),
        vmem((channels, rows), F32),
        vmem((channels, rows), F32),
        vmem((channels, rows), F32),
        vmem((channels, rows), F32),
        vmem((cts, rows, LANES), F32),
        vmem((groups, 2 * LANES, LANES), BF16),
        vmem((groups, LANES, 2 * LANES), BF16),
        vmem((groups, LANES, LANES), BF16),
        vmem((channels, long), F32),
        vmem((channels, LANES), F32),
        vmem((blocks, LANES, LANES), F32),
        vmem((blocks, LANES, LANES), F32),
        vmem((n_dp, 8, LANES), F32),
        vmem((64, LANES), F32),
        vmem((n_y, mine, LANES), F32),
        vmem((n_z, mine, LANES), F32),
        vmem((n_y, mine, LANES), F32),
        dma((5,)), dma((2,)), dma((2,)),
        dma((n_dp,)), dma((n_dp,)),
        dma((n_y,)), dma((n_y,)),
        dma((n_z,)), dma((n_z,)),
        dma((n_y,)), dma((n_y,)),
    ]
    anywhere = pl.BlockSpec(memory_space=pl.ANY)
    inside = pl.BlockSpec(memory_space=pltpu.VMEM)
    feat, filt, skip = pl.pallas_call(
        functools.partial(kernel, geo),
        out_shape=(
            jax.ShapeDtypeStruct((3, n_taps, channels), F32),
            jax.ShapeDtypeStruct((groups, filter_taps), F32),
            jax.ShapeDtypeStruct((1, channels), F32),
        ),
        in_specs=[anywhere] * 5,
        out_specs=(inside,) * 3,
        scratch_shapes=scratch,
        compiler_params=pltpu.CompilerParams(
            collective_id=0, has_side_effects=True, vmem_limit_bytes=48 * 1024 * 1024),
    )(projected, featurizer.transpose(1, 0, 2), long_filter, skip_gain.reshape(1, channels), out_cotangent)
    return feat.transpose(1, 0, 2), filt, skip.reshape(channels)


def solution(mesh):
    sizes = (mesh.shape["seq"], mesh.shape["dp"])
    return jax.shard_map(
        functools.partial(body, sizes),
        mesh=mesh,
        in_specs=(
            P(None, "seq", "dp"),
            P(None, None, "dp"),
            P("dp", None),
            P("dp"),
            P("seq", "dp"),
        ),
        out_specs=(P(None, None, "dp"), P("dp", None), P("dp")),
        check_vma=False,
    )
```

```python
import functools
import math

import jax
import jax.numpy as jnp
from jax import lax
from jax.experimental import pallas as pl
from jax.experimental.pallas import tpu as pltpu
from jax.sharding import PartitionSpec as P

F32 = jnp.float32
BF16 = jnp.bfloat16
LANES = 128
MEMBERS = 16
HALO = 144
MESH = pl.DeviceIdType.MESH


def iota(shape, dim):
    return lax.broadcasted_iota(jnp.int32, shape, dim)


def dot(lhs, rhs):
    return lax.dot_general(lhs, rhs, (((1,), (0,)), ((), ())), preferred_element_type=F32)


def dot_nt(lhs, rhs):
    return lax.dot_general(lhs, rhs, (((1,), (1,)), ((), ())), preferred_element_type=F32)


def aligned(index, step):
    return pl.multiple_of(index * step, step)


def fold(array):
    total = array[0:8]
    for begin in range(8, array.shape[0], 8):
        total = total + array[begin : begin + 8]
    return total


def kernel(geo, proj, taps, filt, skip, cot, out_f, out_l, out_s,
           pb, cb, tr, lf, sk, lff, wv, pf, kv, qv, xt, qt, gt, innt, ut, wt, inn, tof, tob, xg,
           pgt, skt, at, bt, st, acc, bases, slr, sly, slz,
           ld_sem, h_s, h_r, s_s, s_r, a_s, a_r, b_s, b_r, c_s, c_r):
    n_seq, n_dp, n_y, n_z, rows, n_taps, channels = geo
    blocks = rows // LANES
    groups = channels // MEMBERS
    cts = channels // LANES
    me = lax.axis_index("seq")
    md = lax.axis_index("dp")
    my = me // n_z
    mz = lax.rem(me, n_z)
    core = lax.rem(mz, 2)
    half = 32

    loads = [
        pltpu.make_async_copy(filt, lf, ld_sem.at[0]),
        pltpu.make_async_copy(taps, tr, ld_sem.at[1]),
        pltpu.make_async_copy(skip, sk, ld_sem.at[2]),
        pltpu.make_async_copy(proj, pb.at[:, pl.ds(HALO, rows), :], ld_sem.at[3]),
        pltpu.make_async_copy(cot, cb, ld_sem.at[4]),
    ]
    for copy in loads:
        copy.start()

    barrier = pltpu.get_barrier_semaphore()

    def dp_peer(i):
        return {"dp": lax.rem(md + i, n_dp)}

    def y_index(i):
        return lax.rem(my + i, n_y)

    def y_peer(i):
        return {"seq": y_index(i) * n_z + mz}

    def z_peer(i):
        return {"seq": my * n_z + lax.rem(mz + i, n_z)}

    def greet(peer, count):
        @pl.loop(1, count)
        def _(i):
            pl.semaphore_signal(barrier, 1, device_id=peer(i), device_id_type=MESH)

    ahead = {"seq": lax.rem(me + 1, n_seq)}
    behind = {"seq": lax.rem(me + n_seq - 1, n_seq)}
    pl.semaphore_signal(barrier, 1, device_id=behind, device_id_type=MESH)
    pl.semaphore_signal(barrier, 1, device_id=ahead, device_id_type=MESH)
    greet(dp_peer, n_dp)
    greet(y_peer, n_y)
    greet(z_peer, n_z)

    for copy in loads[:3]:
        copy.wait()
    for p in range(3):
        wv[p, 0:n_taps, :] = tr[p].astype(F32)

    def featured(p, ct, block):
        window = pf.at[p * cts + ct, pl.ds(aligned(block, LANES), LANES + 16), :]
        total = None
        for j in range(n_taps):
            term = wv[p, j : j + 1, ct * LANES : (ct + 1) * LANES] * window[16 - j : 16 - j + LANES, :]
            total = term if total is None else total + term
        return total.astype(BF16).astype(F32)

    def widen(begin, count):
        for p in range(3):
            for ct in range(cts):
                pf[p * cts + ct, pl.ds(begin, count), :] = pb[
                    p, pl.ds(begin, count), ct * LANES : (ct + 1) * LANES].astype(F32)

    def product_block(block):
        for ct in range(cts):
            cols = slice(ct * LANES, (ct + 1) * LANES)
            here = pl.ds(aligned(block, LANES), LANES)
            keys = featured(1, ct, block)
            values = featured(2, ct, block)
            kv[ct, here, :] = keys
            kv[cts + ct, here, :] = values
            product = (keys * values).astype(BF16)
            xt[cols, here] = product.astype(F32).T.astype(BF16)

    def query_block(block):
        for ct in range(cts):
            cols = slice(ct * LANES, (ct + 1) * LANES)
            inside = pl.ds(aligned(block - 1, LANES), LANES)
            queries = featured(0, ct, block)
            qv[ct, inside, :] = queries
            qt[cols, inside] = queries.T
            gt[cols, inside] = cb[inside, cols].astype(F32).T

    loads[3].wait()

    @pl.loop(0, blocks)
    def _(block):
        widen(pl.multiple_of(HALO + block * LANES, 16), LANES)

    product_block(blocks)

    pl.semaphore_wait(barrier, n_dp + n_y + n_z - 1)

    def rim(number, src, dst):
        return pltpu.make_async_remote_copy(
            src_ref=src, dst_ref=dst, send_sem=h_s.at[number], recv_sem=h_r.at[number],
            device_id=ahead, device_id_type=MESH)

    halo = [
        rim(0, proj.at[:, pl.ds(rows - 16, 16), :], pb.at[:, pl.ds(HALO - 16, 16), :]),
        rim(1, xt.at[:, pl.ds(rows, LANES)], xt.at[:, pl.ds(0, LANES)]),
        rim(2, proj.at[pl.ds(1, 2), pl.ds(rows - HALO, LANES), :],
            pb.at[pl.ds(1, 2), pl.ds(0, LANES), :]),
    ]

    @pl.when(me < n_seq - 1)
    def _():
        for copy in halo:
            copy.start()

    loads[4].wait()

    @pl.loop(2, blocks)
    def _(block):
        product_block(block)

    @pl.loop(2, blocks + 1)
    def _(block):
        query_block(block)

    lff[...] = lf[...].astype(F32)
    row8 = iota((8, LANES), 0)
    row_all = iota((8 * groups, LANES), 0)
    keep = iota((LANES, LANES), 1) >= iota((LANES, LANES), 0)
    base = jnp.concatenate(
        [jnp.broadcast_to(lff[g : g + 1, :], (8, LANES)) for g in range(groups)], axis=0)
    for k in (1, 2, 4):
        base = jnp.where((row_all & k) != 0, pltpu.roll(base, k, 1), base)
    bases[...] = base

    def toeplitz(g, carry):
        base = bases[pl.ds(aligned(g, 8), 8), :]
        tiles = [base] + [pltpu.roll(base, 8 * r, 1) for r in range(1, LANES // 8)]
        circ = jnp.concatenate(tiles, axis=0)
        near = jnp.where(keep, circ, 0.0).astype(BF16)
        far = jnp.where(keep, 0.0, circ).astype(BF16)
        tof[g, 0:LANES, :] = far
        tof[g, LANES : 2 * LANES, :] = near
        tob[g, :, 0:LANES] = near
        tob[g, :, LANES : 2 * LANES] = far
        return carry

    lax.fori_loop(0, groups, toeplitz, 0, unroll=4)

    for ct in range(cts):
        cols = slice(ct * LANES, (ct + 1) * LANES)
        line = jnp.broadcast_to(sk[ct : ct + 1, :].astype(F32), (LANES, LANES))
        skt[cols, :] = line.T

    @pl.when(me > 0)
    def _():
        halo[0].wait_recv()

    @pl.when(me == 0)
    def _():
        pb[:, 0:HALO, :] = jnp.zeros((3, HALO, channels), BF16)
        xt[:, 0:LANES] = jnp.zeros((channels, LANES), BF16)

    widen(HALO - 16, 16)
    product_block(1)
    query_block(1)

    @pl.when(me > 0)
    def _():
        halo[1].wait_recv()

    zero8 = jnp.zeros((8, LANES), F32)

    def forward(g, sums):
        sums = list(sums)
        r = pl.ds(aligned(g, MEMBERS), MEMBERS)
        source = [xt[r, b * LANES : (b + 1) * LANES] for b in range(blocks + 1)]
        left = jnp.concatenate(
            [jnp.concatenate([source[b], source[b + 1]], axis=1) for b in range(blocks)], axis=0)
        filtered = dot(left, tof[g])
        gain = skt[r, :]
        for b in range(blocks):
            cols = slice(b * LANES, (b + 1) * LANES)
            inner = filtered[b * MEMBERS : (b + 1) * MEMBERS] + gain * source[b + 1].astype(F32)
            queries = qt[r, cols]
            output = queries * inner
            cotangent = gt[r, cols]
            sums[b] = sums[b] + fold(output * output)
            sums[blocks + b] = sums[blocks + b] + fold(cotangent * output)
            innt[r, cols] = inner
            ut[r, cols] = cotangent * queries
            wt[r, cols] = output * queries
        return tuple(sums)

    sums = lax.fori_loop(0, groups, forward, (zero8,) * (2 * blocks), unroll=4)
    st[md] = jnp.concatenate([jnp.sum(part, axis=0, keepdims=True) for part in sums], axis=0)

    def stat_copy(i):
        return pltpu.make_async_remote_copy(
            src_ref=st.at[md], dst_ref=st.at[md], send_sem=s_s.at[i],
            recv_sem=s_r.at[md], device_id=dp_peer(i), device_id_type=MESH)

    @pl.loop(1, n_dp)
    def _(i):
        stat_copy(i).start()

    @pl.loop(0, blocks)
    def _(block):
        here = pl.ds(aligned(block, LANES), LANES)
        for ct in range(cts):
            inn[ct, here, :] = innt[ct * LANES : (ct + 1) * LANES, here].T

    @pl.loop(0, groups)
    def _(g):
        r = pl.ds(aligned(g, MEMBERS), MEMBERS)
        stack = [xt[r, b * LANES : (b + 1) * LANES].astype(F32) for b in range(blocks + 1)]
        stack.append(jnp.zeros((LANES - (blocks + 1) * MEMBERS, LANES), F32))
        xg[g] = jnp.concatenate(stack, axis=0).T.astype(BF16)

    @pl.when(me > 0)
    def _():
        halo[2].wait_recv()

    widen(0, LANES)
    for ct in range(cts):
        for p in (1, 2):
            kv[(p - 1) * cts + ct, 0:LANES, :] = featured(p, ct, 0)

    @pl.loop(1, n_dp)
    def _(i):
        src = lax.rem(md + i, n_dp)
        pltpu.make_async_remote_copy(
            src_ref=st.at[src], dst_ref=st.at[src], send_sem=s_s.at[i],
            recv_sem=s_r.at[src], device_id=dp_peer(i), device_id_type=MESH).wait_recv()

    whole = st[0]
    for i in range(1, n_dp):
        whole = whole + st[i]
    mean = whole * (1.0 / (channels * n_dp))
    token_scale = 1.0 / math.sqrt(rows * n_seq)
    rms = jnp.sqrt(mean[0:blocks] + 1e-05)
    scale_a = token_scale / rms
    scale_b = token_scale * mean[blocks : 2 * blocks] / (rms * rms * rms)
    lines_a = [scale_a[b : b + 1] for b in range(blocks)]
    lines_b = [scale_b[b : b + 1] for b in range(blocks)]
    for b in range(blocks):
        at[b] = jnp.broadcast_to(lines_a[b], (LANES, LANES)).T
        bt[b] = jnp.broadcast_to(lines_b[b], (LANES, LANES)).T

    pad = jnp.zeros((MEMBERS, LANES), BF16)
    fill = jnp.zeros((LANES - (blocks + 1) * MEMBERS, LANES), BF16)

    def backward(g, carry):
        r = pl.ds(aligned(g, MEMBERS), MEMBERS)
        parts = []
        for b in range(blocks):
            cols = slice(b * LANES, (b + 1) * LANES)
            parts.append((ut[r, cols] * lines_a[b] - wt[r, cols] * lines_b[b]).astype(BF16))
        chain = [pad] + parts + [pad]
        left = jnp.concatenate(
            [jnp.concatenate([chain[b], chain[b + 1]], axis=1) for b in range(blocks + 1)], axis=0)
        grad = dot_nt(left, tob[g])
        for b in range(blocks + 1):
            pgt[r, b * LANES : (b + 1) * LANES] = grad[b * MEMBERS : (b + 1) * MEMBERS]
        right = jnp.concatenate(
            [jnp.concatenate(parts + [pad, fill], axis=0), jnp.concatenate([pad] + parts + [fill], axis=0)],
            axis=1)
        lagged = dot(xg[g], right)
        square = jnp.where(keep, lagged[:, LANES:], lagged[:, :LANES])
        total = square[0:8]
        for t in range(1, LANES // 8):
            total = total + pltpu.roll(square[8 * t : 8 * t + 8], LANES - 8 * t, 1)
        bases[pl.ds(aligned(g, 8), 8), :] = total
        return carry

    lax.fori_loop(0, groups, backward, 0, unroll=4)
    lag = bases[...]
    for k in (1, 2, 4):
        lag = jnp.where((row_all & k) != 0, pltpu.roll(lag, LANES - k, 1), lag)
    acc[48 : 48 + groups, :] = jnp.concatenate(
        [jnp.sum(lag[8 * g : 8 * g + 8], axis=0, keepdims=True) for g in range(groups)], axis=0)

    for ct in range(cts):
        cols = slice(ct * LANES, (ct + 1) * LANES)
        gain = sk[ct : ct + 1, :].astype(F32)

        def taps_of(part, window, begin, count, grad, totals):
            for j in range(n_taps):
                term = grad * window[16 - j + begin : 16 - j + begin + count, :]
                totals[part * 8 + j] = totals[part * 8 + j] + fold(term)

        def tail(block, totals, inside):
            totals = list(totals)
            here = pl.ds(aligned(block, LANES), LANES)
            backed = pgt[cols, here].T
            windows = [
                pf.at[p * cts + ct, pl.ds(aligned(block, LANES), LANES + 16), :] for p in range(3)]
            step = 32
            for begin in range(0, LANES, step):
                local = pl.ds(pl.multiple_of(block * LANES + begin, 8), step)
                keys = kv[ct, local, :]
                values = kv[cts + ct, local, :]
                grad = backed[begin : begin + step]
                if inside:
                    own = pl.ds(pl.multiple_of((block - 1) * LANES + begin, 16), step)
                    queries = qv[ct, own, :]
                    inner = inn[ct, own, :]
                    first = at[block - 1, begin : begin + step, :]
                    second = bt[block - 1, begin : begin + step, :]
                    out_grad = cb[own, cols].astype(F32) * first - queries * inner * second
                    conv = out_grad * queries
                    grad = grad + gain * conv
                    product = (keys * values).astype(BF16).astype(F32)
                    totals[7] = totals[7] + fold(conv * product)
                    taps_of(0, windows[0], begin, step, out_grad * inner, totals)
                taps_of(1, windows[1], begin, step, grad * values, totals)
                taps_of(2, windows[2], begin, step, grad * keys, totals)
            return tuple(totals)

        totals = tail(0, (zero8,) * 24, False)
        totals = lax.fori_loop(1, blocks + 1, functools.partial(tail, inside=True), totals)
        for p in range(3):
            acc[(p * cts + ct) * 8 : (p * cts + ct) * 8 + 8, :] = jnp.concatenate(
                [jnp.sum(totals[p * 8 + j], axis=0, keepdims=True) for j in range(8)], axis=0)

    partner = {"seq": me + 1 - 2 * core}
    swap = pltpu.make_async_remote_copy(
        src_ref=acc.at[pl.ds(aligned(1 - core, half), half), :], dst_ref=slr,
        send_sem=a_s.at[0], recv_sem=a_r.at[0], device_id=partner, device_id_type=MESH)
    swap.start()

    def z_index(i):
        return lax.rem(mz + i, n_z)

    def exchange(slots, sends, receives, place, i, peer):
        return pltpu.make_async_remote_copy(
            src_ref=slots.at[place], dst_ref=slots.at[place], send_sem=sends.at[i],
            recv_sem=receives.at[place], device_id=peer(i), device_id_type=MESH)

    swap.wait_recv()
    sly[my] = (acc[pl.ds(aligned(core, half), half), :] + slr[...]).astype(BF16)

    @pl.loop(1, n_y)
    def _(i):
        exchange(sly, b_s, b_r, my, i, y_peer).start()

    @pl.loop(1, n_y)
    def _(i):
        exchange(sly, b_s, b_r, y_index(i), i, y_peer).wait_recv()

    part = sly[0].astype(F32)
    for i in range(1, n_y):
        part = part + sly[i].astype(F32)
    slz[mz] = part.astype(BF16)

    @pl.loop(1, n_z)
    def _(i):
        exchange(slz, c_s, c_r, mz, i, z_peer).start()

    @pl.loop(1, n_z)
    def _(i):
        exchange(slz, c_s, c_r, z_index(i), i, z_peer).wait_recv()

    halves = []
    for h in range(2):
        part = slz[h].astype(F32)
        for i in range(1, n_z // 2):
            part = part + slz[2 * i + h].astype(F32)
        halves.append(part)

    def tile(number):
        return halves[number // 4][number % 4 * 8 : number % 4 * 8 + 8]

    for ct in range(cts):
        cols = slice(ct * LANES, (ct + 1) * LANES)
        for p in range(3):
            out_f[p, :, cols] = tile(p * cts + ct)[0:n_taps]
        out_s[:, cols] = tile(ct)[7:8]
    out_l[0:8, :] = tile(6)
    out_l[8:16, :] = tile(7)

    @pl.loop(1, n_dp)
    def _(i):
        stat_copy(i).wait_send()

    swap.wait_send()

    @pl.loop(1, n_y)
    def _(i):
        exchange(sly, b_s, b_r, my, i, y_peer).wait_send()

    @pl.loop(1, n_z)
    def _(i):
        exchange(slz, c_s, c_r, mz, i, z_peer).wait_send()

    @pl.when(me < n_seq - 1)
    def _():
        for copy in halo:
            copy.wait_send()


def body(sizes, projected, featurizer, long_filter, skip_gain, out_cotangent):
    n_seq, n_dp = sizes
    parts, rows, channels = projected.shape
    n_taps = featurizer.shape[0]
    groups, filter_taps = long_filter.shape
    n_y = 1 << ((n_seq.bit_length() - 1) // 2)
    n_z = n_seq // n_y
    blocks = rows // LANES
    cts = channels // LANES
    geo = (n_seq, n_dp, n_y, n_z, rows, n_taps, channels)
    long = rows + LANES
    vmem = pltpu.VMEM
    dma = pltpu.SemaphoreType.DMA
    scratch = [
        vmem((3, HALO + rows, channels), BF16),
        vmem((rows, channels), BF16),
        vmem((3, n_taps, channels), BF16),
        vmem((groups, LANES), BF16),
        vmem((cts, LANES), BF16),
        vmem((groups, LANES), F32),
        vmem((3, 8, channels), F32),
        vmem((3 * cts, HALO + rows, LANES), F32),
        vmem((2 * cts, long, LANES), F32),
        vmem((cts, rows, LANES), F32),
        vmem((channels, long), BF16),
        vmem((channels, rows), F32),
        vmem((channels, rows), F32),
        vmem((channels, rows), F32),
        vmem((channels, rows), F32),
        vmem((channels, rows), F32),
        vmem((cts, rows, LANES), F32),
        vmem((groups, 2 * LANES, LANES), BF16),
        vmem((groups, LANES, 2 * LANES), BF16),
        vmem((groups, LANES, LANES), BF16),
        vmem((channels, long), F32),
        vmem((channels, LANES), F32),
        vmem((blocks, LANES, LANES), F32),
        vmem((blocks, LANES, LANES), F32),
        vmem((n_dp, 8, LANES), F32),
        vmem((64, LANES), F32),
        vmem((8 * groups, LANES), F32),
        vmem((32, LANES), F32),
        vmem((n_y, 32, LANES), BF16),
        vmem((n_z, 32, LANES), BF16),
        dma((5,)), dma((3,)), dma((3,)),
        dma((n_dp,)), dma((n_dp,)),
        dma((1,)), dma((1,)),
        dma((n_y,)), dma((n_y,)),
        dma((n_z,)), dma((n_z,)),
    ]
    anywhere = pl.BlockSpec(memory_space=pl.ANY)
    inside = pl.BlockSpec(memory_space=pltpu.VMEM)
    feat, filt, skip = pl.pallas_call(
        functools.partial(kernel, geo),
        out_shape=(
            jax.ShapeDtypeStruct((3, n_taps, channels), F32),
            jax.ShapeDtypeStruct((groups, filter_taps), F32),
            jax.ShapeDtypeStruct((1, channels), F32),
        ),
        in_specs=[anywhere] * 5,
        out_specs=(inside,) * 3,
        scratch_shapes=scratch,
        compiler_params=pltpu.CompilerParams(
            collective_id=0, has_side_effects=True, vmem_limit_bytes=60 * 1024 * 1024),
    )(projected, featurizer.transpose(1, 0, 2), long_filter, skip_gain.reshape(cts, LANES), out_cotangent)
    return feat.transpose(1, 0, 2), filt, skip.reshape(channels)


def solution(mesh):
    sizes = (mesh.shape["seq"], mesh.shape["dp"])
    return jax.shard_map(
        functools.partial(body, sizes),
        mesh=mesh,
        in_specs=(
            P(None, "seq", "dp"),
            P(None, None, "dp"),
            P("dp", None),
            P("dp"),
            P("seq", "dp"),
        ),
        out_specs=(P(None, None, "dp"), P("dp", None), P("dp")),
        check_vma=False,
    )
```

```python
import functools
import math

import jax
import jax.numpy as jnp
from jax import lax
from jax.experimental import pallas as pl
from jax.experimental.pallas import tpu as pltpu
from jax.sharding import PartitionSpec as P

F32 = jnp.float32
BF16 = jnp.bfloat16
LANES = 128
MEMBERS = 16
HALO = 144
MESH = pl.DeviceIdType.MESH


def iota(shape, dim):
    return lax.broadcasted_iota(jnp.int32, shape, dim)


def dot(lhs, rhs):
    return lax.dot_general(lhs, rhs, (((1,), (0,)), ((), ())), preferred_element_type=F32)


def dot_nt(lhs, rhs):
    return lax.dot_general(lhs, rhs, (((1,), (1,)), ((), ())), preferred_element_type=F32)


def aligned(index, step):
    return pl.multiple_of(index * step, step)


def fold(array):
    total = array[0:8]
    for begin in range(8, array.shape[0], 8):
        total = total + array[begin : begin + 8]
    return total


def kernel(geo, proj, taps, filt, skip, cot, out,
           pb, cb, tr, lf, sk, lff, wv, pf, kv, qv, xt, qt, gt, innt, ut, wt, inn, tof, tob, xg,
           pgt, skt, at, bt, st, acc, bases, slr, sly, slz,
           ld_sem, h_s, h_r, s_s, s_r, a_s, a_r, b_s, b_r, c_s, c_r):
    n_seq, n_dp, n_y, n_z, rows, n_taps, channels = geo
    blocks = rows // LANES
    groups = channels // MEMBERS
    cts = channels // LANES
    me = lax.axis_index("seq")
    md = lax.axis_index("dp")
    my = me // n_z
    mz = lax.rem(me, n_z)
    core = lax.rem(mz, 2)
    half = 32

    loads = [
        pltpu.make_async_copy(filt, lf, ld_sem.at[0]),
        pltpu.make_async_copy(taps, tr, ld_sem.at[1]),
        pltpu.make_async_copy(skip, sk, ld_sem.at[2]),
        pltpu.make_async_copy(proj, pb.at[:, pl.ds(HALO, rows), :], ld_sem.at[3]),
        pltpu.make_async_copy(cot, cb, ld_sem.at[4]),
    ]
    barrier = pltpu.get_barrier_semaphore()

    def dp_peer(i):
        return {"dp": lax.rem(md + i, n_dp)}

    def y_index(i):
        return lax.rem(my + i, n_y)

    def y_peer(i):
        return {"seq": y_index(i) * n_z + mz}

    def z_peer(i):
        return {"seq": my * n_z + lax.rem(mz + i, n_z)}

    def greet(peer, count):
        @pl.loop(1, count)
        def _(i):
            pl.semaphore_signal(barrier, 1, device_id=peer(i), device_id_type=MESH)

    ahead = {"seq": lax.rem(me + 1, n_seq)}
    behind = {"seq": lax.rem(me + n_seq - 1, n_seq)}
    pl.semaphore_signal(barrier, 1, device_id=behind, device_id_type=MESH)
    pl.semaphore_signal(barrier, 1, device_id=ahead, device_id_type=MESH)
    for copy in loads:
        copy.start()
    greet(dp_peer, n_dp)
    greet(y_peer, n_y)
    greet(z_peer, n_z)

    for copy in loads[:3]:
        copy.wait()
    for p in range(3):
        wv[p, 0:n_taps, :] = tr[p].astype(F32)

    def featured(p, ct, block):
        window = pf.at[p * cts + ct, pl.ds(aligned(block, LANES), LANES + 16), :]
        total = None
        for j in range(n_taps):
            term = wv[p, j : j + 1, ct * LANES : (ct + 1) * LANES] * window[16 - j : 16 - j + LANES, :]
            total = term if total is None else total + term
        return total.astype(BF16).astype(F32)

    def widen(begin, count):
        for p in range(3):
            for ct in range(cts):
                pf[p * cts + ct, pl.ds(begin, count), :] = pb[
                    p, pl.ds(begin, count), ct * LANES : (ct + 1) * LANES].astype(F32)

    def product_block(block):
        for ct in range(cts):
            cols = slice(ct * LANES, (ct + 1) * LANES)
            here = pl.ds(aligned(block, LANES), LANES)
            keys = featured(1, ct, block)
            values = featured(2, ct, block)
            kv[ct, here, :] = keys
            kv[cts + ct, here, :] = values
            product = (keys * values).astype(BF16)
            xt[cols, here] = product.astype(F32).T.astype(BF16)

    def query_block(block):
        for ct in range(cts):
            cols = slice(ct * LANES, (ct + 1) * LANES)
            inside = pl.ds(aligned(block - 1, LANES), LANES)
            queries = featured(0, ct, block)
            qv[ct, inside, :] = queries
            qt[cols, inside] = queries.T
            gt[cols, inside] = cb[inside, cols].astype(F32).T

    loads[3].wait()

    @pl.loop(0, blocks)
    def _(block):
        widen(pl.multiple_of(HALO + block * LANES, 16), LANES)

    product_block(blocks)

    pl.semaphore_wait(barrier, n_dp + n_y + n_z - 1)

    def rim(number, src, dst):
        return pltpu.make_async_remote_copy(
            src_ref=src, dst_ref=dst, send_sem=h_s.at[number], recv_sem=h_r.at[number],
            device_id=ahead, device_id_type=MESH)

    halo = [
        rim(0, proj.at[:, pl.ds(rows - 16, 16), :], pb.at[:, pl.ds(HALO - 16, 16), :]),
        rim(1, xt.at[:, pl.ds(rows, LANES)], xt.at[:, pl.ds(0, LANES)]),
        rim(2, proj.at[pl.ds(1, 2), pl.ds(rows - HALO, LANES), :],
            pb.at[pl.ds(1, 2), pl.ds(0, LANES), :]),
    ]

    @pl.when(me < n_seq - 1)
    def _():
        halo[0].start()
        halo[1].start()

    loads[4].wait()

    @pl.loop(2, blocks)
    def _(block):
        product_block(block)

    @pl.loop(2, blocks + 1)
    def _(block):
        query_block(block)

    lff[...] = lf[...].astype(F32)
    row8 = iota((8, LANES), 0)
    row_all = iota((8 * groups, LANES), 0)
    keep = iota((LANES, LANES), 1) >= iota((LANES, LANES), 0)
    base = jnp.concatenate(
        [jnp.broadcast_to(lff[g : g + 1, :], (8, LANES)) for g in range(groups)], axis=0)
    for k in (1, 2, 4):
        base = jnp.where((row_all & k) != 0, pltpu.roll(base, k, 1), base)
    bases[...] = base

    def toeplitz(g, carry):
        base = bases[pl.ds(aligned(g, 8), 8), :]
        tiles = [base] + [pltpu.roll(base, 8 * r, 1) for r in range(1, LANES // 8)]
        circ = jnp.concatenate(tiles, axis=0)
        near = jnp.where(keep, circ, 0.0).astype(BF16)
        far = jnp.where(keep, 0.0, circ).astype(BF16)
        tof[g, 0:LANES, :] = far
        tof[g, LANES : 2 * LANES, :] = near
        tob[g, :, 0:LANES] = near
        tob[g, :, LANES : 2 * LANES] = far
        return carry

    lax.fori_loop(0, groups, toeplitz, 0, unroll=4)

    for ct in range(cts):
        cols = slice(ct * LANES, (ct + 1) * LANES)
        line = jnp.broadcast_to(sk[ct : ct + 1, :].astype(F32), (LANES, LANES))
        skt[cols, :] = line.T

    @pl.when(me > 0)
    def _():
        halo[0].wait_recv()

    @pl.when(me == 0)
    def _():
        pb[:, 0:HALO, :] = jnp.zeros((3, HALO, channels), BF16)
        xt[:, 0:LANES] = jnp.zeros((channels, LANES), BF16)

    widen(HALO - 16, 16)
    product_block(1)
    query_block(1)

    @pl.when(me < n_seq - 1)
    def _():
        halo[2].start()

    @pl.when(me > 0)
    def _():
        halo[1].wait_recv()

    zero8 = jnp.zeros((8, LANES), F32)

    def forward(g, sums):
        sums = list(sums)
        r = pl.ds(aligned(g, MEMBERS), MEMBERS)
        source = [xt[r, b * LANES : (b + 1) * LANES] for b in range(blocks + 1)]
        left = jnp.concatenate(
            [jnp.concatenate([source[b], source[b + 1]], axis=1) for b in range(blocks)], axis=0)
        filtered = dot(left, tof[g])
        gain = skt[r, :]
        for b in range(blocks):
            cols = slice(b * LANES, (b + 1) * LANES)
            inner = filtered[b * MEMBERS : (b + 1) * MEMBERS] + gain * source[b + 1].astype(F32)
            queries = qt[r, cols]
            output = queries * inner
            cotangent = gt[r, cols]
            sums[b] = sums[b] + fold(output * output)
            sums[blocks + b] = sums[blocks + b] + fold(cotangent * output)
            innt[r, cols] = inner
            ut[r, cols] = cotangent * queries
            wt[r, cols] = output * queries
        return tuple(sums)

    sums = lax.fori_loop(0, groups, forward, (zero8,) * (2 * blocks), unroll=8)
    st[md] = jnp.concatenate([jnp.sum(part, axis=0, keepdims=True) for part in sums], axis=0)

    def stat_copy(i):
        return pltpu.make_async_remote_copy(
            src_ref=st.at[md], dst_ref=st.at[md], send_sem=s_s.at[i],
            recv_sem=s_r.at[md], device_id=dp_peer(i), device_id_type=MESH)

    @pl.loop(1, n_dp)
    def _(i):
        stat_copy(i).start()

    @pl.loop(0, blocks)
    def _(block):
        here = pl.ds(aligned(block, LANES), LANES)
        for ct in range(cts):
            inn[ct, here, :] = innt[ct * LANES : (ct + 1) * LANES, here].T

    @pl.loop(0, groups)
    def _(g):
        r = pl.ds(aligned(g, MEMBERS), MEMBERS)
        stack = [xt[r, b * LANES : (b + 1) * LANES].astype(F32) for b in range(blocks + 1)]
        stack.append(jnp.zeros((LANES - (blocks + 1) * MEMBERS, LANES), F32))
        xg[g] = jnp.concatenate(stack, axis=0).T.astype(BF16)

    @pl.when(me > 0)
    def _():
        halo[2].wait_recv()

    widen(0, LANES)
    for ct in range(cts):
        for p in (1, 2):
            kv[(p - 1) * cts + ct, 0:LANES, :] = featured(p, ct, 0)

    @pl.loop(1, n_dp)
    def _(i):
        src = lax.rem(md + i, n_dp)
        pltpu.make_async_remote_copy(
            src_ref=st.at[src], dst_ref=st.at[src], send_sem=s_s.at[i],
            recv_sem=s_r.at[src], device_id=dp_peer(i), device_id_type=MESH).wait_recv()

    whole = st[0]
    for i in range(1, n_dp):
        whole = whole + st[i]
    mean = whole * (1.0 / (channels * n_dp))
    token_scale = 1.0 / math.sqrt(rows * n_seq)
    rms = jnp.sqrt(mean[0:blocks] + 1e-05)
    scale_a = token_scale / rms
    scale_b = token_scale * mean[blocks : 2 * blocks] / (rms * rms * rms)
    lines_a = [scale_a[b : b + 1] for b in range(blocks)]
    lines_b = [scale_b[b : b + 1] for b in range(blocks)]
    for b in range(blocks):
        at[b] = jnp.broadcast_to(lines_a[b], (LANES, LANES)).T
        bt[b] = jnp.broadcast_to(lines_b[b], (LANES, LANES)).T

    pad = jnp.zeros((MEMBERS, LANES), BF16)
    fill = jnp.zeros((LANES - (blocks + 1) * MEMBERS, LANES), BF16)

    def backward(g, carry):
        r = pl.ds(aligned(g, MEMBERS), MEMBERS)
        parts = []
        for b in range(blocks):
            cols = slice(b * LANES, (b + 1) * LANES)
            parts.append((ut[r, cols] * lines_a[b] - wt[r, cols] * lines_b[b]).astype(BF16))
        chain = [pad] + parts + [pad]
        left = jnp.concatenate(
            [jnp.concatenate([chain[b], chain[b + 1]], axis=1) for b in range(blocks + 1)], axis=0)
        grad = dot_nt(left, tob[g])
        for b in range(blocks + 1):
            pgt[r, b * LANES : (b + 1) * LANES] = grad[b * MEMBERS : (b + 1) * MEMBERS]
        right = jnp.concatenate(
            [jnp.concatenate(parts + [pad, fill], axis=0), jnp.concatenate([pad] + parts + [fill], axis=0)],
            axis=1)
        lagged = dot(xg[g], right)
        square = jnp.where(keep, lagged[:, LANES:], lagged[:, :LANES])
        total = square[0:8]
        for t in range(1, LANES // 8):
            total = total + pltpu.roll(square[8 * t : 8 * t + 8], LANES - 8 * t, 1)
        bases[pl.ds(aligned(g, 8), 8), :] = total
        return carry

    lax.fori_loop(0, groups, backward, 0, unroll=8)
    lag = bases[...]
    for k in (1, 2, 4):
        lag = jnp.where((row_all & k) != 0, pltpu.roll(lag, LANES - k, 1), lag)
    acc[48 : 48 + groups, :] = jnp.concatenate(
        [jnp.sum(lag[8 * g : 8 * g + 8], axis=0, keepdims=True) for g in range(groups)], axis=0)

    for ct in range(cts):
        cols = slice(ct * LANES, (ct + 1) * LANES)
        gain = sk[ct : ct + 1, :].astype(F32)

        def taps_of(part, window, begin, count, grad, totals):
            for j in range(n_taps):
                term = grad * window[16 - j + begin : 16 - j + begin + count, :]
                totals[part * 8 + j] = totals[part * 8 + j] + fold(term)

        def tail(block, totals, inside):
            totals = list(totals)
            here = pl.ds(aligned(block, LANES), LANES)
            backed = pgt[cols, here].T
            windows = [
                pf.at[p * cts + ct, pl.ds(aligned(block, LANES), LANES + 16), :] for p in range(3)]
            step = 32
            for begin in range(0, LANES, step):
                local = pl.ds(pl.multiple_of(block * LANES + begin, 8), step)
                keys = kv[ct, local, :]
                values = kv[cts + ct, local, :]
                grad = backed[begin : begin + step]
                if inside:
                    own = pl.ds(pl.multiple_of((block - 1) * LANES + begin, 16), step)
                    queries = qv[ct, own, :]
                    inner = inn[ct, own, :]
                    first = at[block - 1, begin : begin + step, :]
                    second = bt[block - 1, begin : begin + step, :]
                    out_grad = cb[own, cols].astype(F32) * first - queries * inner * second
                    conv = out_grad * queries
                    grad = grad + gain * conv
                    product = (keys * values).astype(BF16).astype(F32)
                    totals[7] = totals[7] + fold(conv * product)
                    taps_of(0, windows[0], begin, step, out_grad * inner, totals)
                taps_of(1, windows[1], begin, step, grad * values, totals)
                taps_of(2, windows[2], begin, step, grad * keys, totals)
            return tuple(totals)

        totals = tail(0, (zero8,) * 24, False)
        totals = lax.fori_loop(1, blocks + 1, functools.partial(tail, inside=True), totals)
        for p in range(3):
            acc[(p * cts + ct) * 8 : (p * cts + ct) * 8 + 8, :] = jnp.concatenate(
                [jnp.sum(totals[p * 8 + j], axis=0, keepdims=True) for j in range(8)], axis=0)

    partner = {"seq": me + 1 - 2 * core}
    swap = pltpu.make_async_remote_copy(
        src_ref=acc.at[pl.ds(aligned(1 - core, half), half), :], dst_ref=slr,
        send_sem=a_s.at[0], recv_sem=a_r.at[0], device_id=partner, device_id_type=MESH)
    swap.start()

    def z_index(i):
        return lax.rem(mz + i, n_z)

    def exchange(slots, sends, receives, place, i, peer):
        return pltpu.make_async_remote_copy(
            src_ref=slots.at[place], dst_ref=slots.at[place], send_sem=sends.at[i],
            recv_sem=receives.at[place], device_id=peer(i), device_id_type=MESH)

    swap.wait_recv()
    sly[my] = (acc[pl.ds(aligned(core, half), half), :] + slr[...]).astype(BF16)

    @pl.loop(1, n_y)
    def _(i):
        exchange(sly, b_s, b_r, my, i, y_peer).start()

    @pl.loop(1, n_y)
    def _(i):
        exchange(sly, b_s, b_r, y_index(i), i, y_peer).wait_recv()

    part = sly[0].astype(F32)
    for i in range(1, n_y):
        part = part + sly[i].astype(F32)
    slz[mz] = part.astype(BF16)

    @pl.loop(1, n_z)
    def _(i):
        exchange(slz, c_s, c_r, mz, i, z_peer).start()

    @pl.loop(1, n_z)
    def _(i):
        exchange(slz, c_s, c_r, z_index(i), i, z_peer).wait_recv()

    for h in range(2):
        part = slz[h].astype(F32)
        for i in range(1, n_z // 2):
            part = part + slz[2 * i + h].astype(F32)
        out[h * half : (h + 1) * half, :] = part

    @pl.loop(1, n_dp)
    def _(i):
        stat_copy(i).wait_send()

    swap.wait_send()

    @pl.loop(1, n_y)
    def _(i):
        exchange(sly, b_s, b_r, my, i, y_peer).wait_send()

    @pl.loop(1, n_z)
    def _(i):
        exchange(slz, c_s, c_r, mz, i, z_peer).wait_send()

    @pl.when(me < n_seq - 1)
    def _():
        for copy in halo:
            copy.wait_send()


def unpack(packed, out_f, out_l, out_s):
    parts, n_taps, channels = out_f.shape
    cts = channels // LANES
    for ct in range(cts):
        cols = slice(ct * LANES, (ct + 1) * LANES)
        for p in range(parts):
            begin = (p * cts + ct) * 8
            out_f[p, :, cols] = packed[begin : begin + n_taps, :]
        out_s[:, cols] = packed[ct * 8 + 7 : ct * 8 + 8, :]
    out_l[...] = packed[parts * cts * 8 :, :]


def body(sizes, projected, featurizer, long_filter, skip_gain, out_cotangent):
    n_seq, n_dp = sizes
    parts, rows, channels = projected.shape
    n_taps = featurizer.shape[0]
    groups, filter_taps = long_filter.shape
    n_y = 1 << ((n_seq.bit_length() - 1) // 2)
    n_z = n_seq // n_y
    blocks = rows // LANES
    cts = channels // LANES
    geo = (n_seq, n_dp, n_y, n_z, rows, n_taps, channels)
    long = rows + LANES
    vmem = pltpu.VMEM
    dma = pltpu.SemaphoreType.DMA
    scratch = [
        vmem((3, HALO + rows, channels), BF16),
        vmem((rows, channels), BF16),
        vmem((3, n_taps, channels), BF16),
        vmem((groups, LANES), BF16),
        vmem((cts, LANES), BF16),
        vmem((groups, LANES), F32),
        vmem((3, 8, channels), F32),
        vmem((3 * cts, HALO + rows, LANES), F32),
        vmem((2 * cts, long, LANES), F32),
        vmem((cts, rows, LANES), F32),
        vmem((channels, long), BF16),
        vmem((channels, rows), F32),
        vmem((channels, rows), F32),
        vmem((channels, rows), F32),
        vmem((channels, rows), F32),
        vmem((channels, rows), F32),
        vmem((cts, rows, LANES), F32),
        vmem((groups, 2 * LANES, LANES), BF16),
        vmem((groups, LANES, 2 * LANES), BF16),
        vmem((groups, LANES, LANES), BF16),
        vmem((channels, long), F32),
        vmem((channels, LANES), F32),
        vmem((blocks, LANES, LANES), F32),
        vmem((blocks, LANES, LANES), F32),
        vmem((n_dp, 8, LANES), F32),
        vmem((64, LANES), F32),
        vmem((8 * groups, LANES), F32),
        vmem((32, LANES), F32),
        vmem((n_y, 32, LANES), BF16),
        vmem((n_z, 32, LANES), BF16),
        dma((5,)), dma((3,)), dma((3,)),
        dma((n_dp,)), dma((n_dp,)),
        dma((1,)), dma((1,)),
        dma((n_y,)), dma((n_y,)),
        dma((n_z,)), dma((n_z,)),
    ]
    inside = pl.BlockSpec(memory_space=pltpu.VMEM)
    packed = pl.pallas_call(
        functools.partial(kernel, geo),
        out_shape=jax.ShapeDtypeStruct((64, LANES), F32),
        in_specs=[pl.BlockSpec(memory_space=pltpu.HBM)] * 5,
        out_specs=inside,
        scratch_shapes=scratch,
        compiler_params=pltpu.CompilerParams(
            collective_id=0, has_side_effects=True, vmem_limit_bytes=60 * 1024 * 1024),
    )(projected, featurizer.transpose(1, 0, 2), long_filter, skip_gain.reshape(cts, LANES), out_cotangent)
    feat, filt, skip = pl.pallas_call(
        unpack,
        out_shape=(
            jax.ShapeDtypeStruct((parts, n_taps, channels), F32),
            jax.ShapeDtypeStruct((groups, filter_taps), F32),
            jax.ShapeDtypeStruct((1, channels), F32),
        ),
        in_specs=[inside],
        out_specs=(inside,) * 3,
        compiler_params=pltpu.CompilerParams(vmem_limit_bytes=60 * 1024 * 1024),
    )(packed)
    return feat.transpose(1, 0, 2), filt, skip.reshape(channels)


def solution(mesh):
    sizes = (mesh.shape["seq"], mesh.shape["dp"])
    return jax.shard_map(
        functools.partial(body, sizes),
        mesh=mesh,
        in_specs=(
            P(None, "seq", "dp"),
            P(None, None, "dp"),
            P("dp", None),
            P("dp"),
            P("seq", "dp"),
        ),
        out_specs=(P(None, None, "dp"), P("dp", None), P("dp")),
        check_vma=False,
    )
```

```python
import functools
import math

import jax
import jax.numpy as jnp
from jax import lax
from jax.experimental import pallas as pl
from jax.experimental.pallas import tpu as pltpu
from jax.sharding import PartitionSpec as P

F32 = jnp.float32
BF16 = jnp.bfloat16
LANES = 128
MEMBERS = 16
HALO = 144
MESH = pl.DeviceIdType.MESH


def iota(shape, dim):
    return lax.broadcasted_iota(jnp.int32, shape, dim)


def dot(lhs, rhs):
    return lax.dot_general(lhs, rhs, (((1,), (0,)), ((), ())), preferred_element_type=F32)


def dot_nt(lhs, rhs):
    return lax.dot_general(lhs, rhs, (((1,), (1,)), ((), ())), preferred_element_type=F32)


def aligned(index, step):
    return pl.multiple_of(index * step, step)


def fold(array):
    total = array[0:8]
    for begin in range(8, array.shape[0], 8):
        total = total + array[begin : begin + 8]
    return total


def kernel(geo, proj, taps, filt, skip, cot, out,
           pb, cb, tr, lf, sk, lff, wv, pf, kv, qv, xt, qt, gt, innt, ut, wt, inn, tof, tob, xg,
           pgt, skt, at, bt, st, st2, acc, tots, bases, slr, sly, slz,
           ld_sem, h_s, h_r, s_s, s_r, t_s, t_r, a_s, a_r, b_s, b_r, c_s, c_r):
    n_seq, n_dp, n_y, n_z, rows, n_taps, channels = geo
    blocks = rows // LANES
    groups = channels // MEMBERS
    cts = channels // LANES
    me = lax.axis_index("seq")
    md = lax.axis_index("dp")
    my = me // n_z
    mz = lax.rem(me, n_z)
    core = lax.rem(mz, 2)
    half = 32

    loads = [
        pltpu.make_async_copy(filt, lf, ld_sem.at[0]),
        pltpu.make_async_copy(taps, tr, ld_sem.at[1]),
        pltpu.make_async_copy(skip, sk, ld_sem.at[2]),
        pltpu.make_async_copy(proj, pb.at[:, pl.ds(HALO, rows), :], ld_sem.at[3]),
        pltpu.make_async_copy(cot, cb, ld_sem.at[4]),
    ]
    barrier = pltpu.get_barrier_semaphore()

    def dp_peer(i):
        return {"dp": lax.rem(md + i, n_dp)}

    def y_index(i):
        return lax.rem(my + i, n_y)

    def y_peer(i):
        return {"seq": y_index(i) * n_z + mz}

    def z_peer(i):
        return {"seq": my * n_z + lax.rem(mz + i, n_z)}

    def greet(peer, count):
        @pl.loop(1, count)
        def _(i):
            pl.semaphore_signal(barrier, 1, device_id=peer(i), device_id_type=MESH)

    ahead = {"seq": lax.rem(me + 1, n_seq)}
    behind = {"seq": lax.rem(me + n_seq - 1, n_seq)}
    pl.semaphore_signal(barrier, 1, device_id=behind, device_id_type=MESH)
    pl.semaphore_signal(barrier, 1, device_id=ahead, device_id_type=MESH)
    for copy in loads:
        copy.start()
    greet(dp_peer, n_dp)
    greet(y_peer, n_y)
    greet(z_peer, n_z)

    for copy in loads[:3]:
        copy.wait()
    for p in range(3):
        wv[p, 0:n_taps, :] = tr[p].astype(F32)

    def featured(p, ct, block):
        window = pf.at[p * cts + ct, pl.ds(aligned(block, LANES), LANES + 16), :]
        total = None
        for j in range(n_taps):
            term = wv[p, j : j + 1, ct * LANES : (ct + 1) * LANES] * window[16 - j : 16 - j + LANES, :]
            total = term if total is None else total + term
        return total.astype(BF16).astype(F32)

    def widen(begin, count):
        for p in range(3):
            for ct in range(cts):
                pf[p * cts + ct, pl.ds(begin, count), :] = pb[
                    p, pl.ds(begin, count), ct * LANES : (ct + 1) * LANES].astype(F32)

    def product_block(block):
        for ct in range(cts):
            cols = slice(ct * LANES, (ct + 1) * LANES)
            here = pl.ds(aligned(block, LANES), LANES)
            keys = featured(1, ct, block)
            values = featured(2, ct, block)
            kv[ct, here, :] = keys
            kv[cts + ct, here, :] = values
            product = (keys * values).astype(BF16)
            xt[cols, here] = product.astype(F32).T.astype(BF16)

    def query_block(block):
        for ct in range(cts):
            cols = slice(ct * LANES, (ct + 1) * LANES)
            inside = pl.ds(aligned(block - 1, LANES), LANES)
            queries = featured(0, ct, block)
            qv[ct, inside, :] = queries
            qt[cols, inside] = queries.T
            gt[cols, inside] = cb[inside, cols].astype(F32).T

    loads[3].wait()

    @pl.loop(0, blocks)
    def _(block):
        widen(pl.multiple_of(HALO + block * LANES, 16), LANES)

    product_block(blocks)

    pl.semaphore_wait(barrier, n_dp + n_y + n_z - 1)

    def rim(number, src, dst):
        return pltpu.make_async_remote_copy(
            src_ref=src, dst_ref=dst, send_sem=h_s.at[number], recv_sem=h_r.at[number],
            device_id=ahead, device_id_type=MESH)

    halo = [
        rim(0, proj.at[:, pl.ds(rows - 16, 16), :], pb.at[:, pl.ds(HALO - 16, 16), :]),
        rim(1, xt.at[:, pl.ds(rows, LANES)], xt.at[:, pl.ds(0, LANES)]),
        rim(2, proj.at[pl.ds(1, 2), pl.ds(rows - HALO, LANES), :],
            pb.at[pl.ds(1, 2), pl.ds(0, LANES), :]),
    ]

    @pl.when(me < n_seq - 1)
    def _():
        halo[0].start()
        halo[1].start()

    loads[4].wait()

    @pl.loop(2, blocks)
    def _(block):
        product_block(block)

    @pl.loop(2, blocks + 1)
    def _(block):
        query_block(block)

    lff[...] = lf[...].astype(F32)
    row_all = iota((8 * groups, LANES), 0)
    keep = iota((LANES, LANES), 1) >= iota((LANES, LANES), 0)
    base = jnp.concatenate(
        [jnp.broadcast_to(lff[g : g + 1, :], (8, LANES)) for g in range(groups)], axis=0)
    for k in (1, 2, 4):
        base = jnp.where((row_all & k) != 0, pltpu.roll(base, k, 1), base)
    bases[...] = base

    def toeplitz(g, carry):
        base = bases[pl.ds(aligned(g, 8), 8), :]
        tiles = [base] + [pltpu.roll(base, 8 * r, 1) for r in range(1, LANES // 8)]
        circ = jnp.concatenate(tiles, axis=0)
        near = jnp.where(keep, circ, 0.0).astype(BF16)
        far = jnp.where(keep, 0.0, circ).astype(BF16)
        tof[g, 0:LANES, :] = far
        tof[g, LANES : 2 * LANES, :] = near
        tob[g, :, 0:LANES] = near
        tob[g, :, LANES : 2 * LANES] = far
        return carry

    lax.fori_loop(0, groups, toeplitz, 0, unroll=4)

    for ct in range(cts):
        cols = slice(ct * LANES, (ct + 1) * LANES)
        line = jnp.broadcast_to(sk[ct : ct + 1, :].astype(F32), (LANES, LANES))
        skt[cols, :] = line.T

    zero8 = jnp.zeros((8, LANES), F32)
    split = blocks // 2

    def forward(begin, end):
        def run(g, sums):
            sums = list(sums)
            r = pl.ds(aligned(g, MEMBERS), MEMBERS)
            source = [xt[r, b * LANES : (b + 1) * LANES] for b in range(begin, end + 1)]
            left = jnp.concatenate(
                [jnp.concatenate(source[b : b + 2], axis=1) for b in range(end - begin)], axis=0)
            filtered = dot(left, tof[g])
            gain = skt[r, :]
            for b in range(end - begin):
                cols = slice((begin + b) * LANES, (begin + b + 1) * LANES)
                inner = filtered[b * MEMBERS : (b + 1) * MEMBERS] + gain * source[b + 1].astype(F32)
                queries = qt[r, cols]
                output = queries * inner
                cotangent = gt[r, cols]
                sums[b] = sums[b] + fold(output * output)
                sums[end - begin + b] = sums[end - begin + b] + fold(cotangent * output)
                innt[r, cols] = inner
                ut[r, cols] = cotangent * queries
                wt[r, cols] = output * queries
            return tuple(sums)

        sums = lax.fori_loop(0, groups, run, (zero8,) * (2 * (end - begin)), unroll=8)
        return jnp.concatenate([jnp.sum(part, axis=0, keepdims=True) for part in sums], axis=0)

    def stat_copy(slots, sends, receives, i, index=None):
        place = md if index is None else index
        return pltpu.make_async_remote_copy(
            src_ref=slots.at[place], dst_ref=slots.at[place], send_sem=sends.at[i],
            recv_sem=receives.at[place], device_id=dp_peer(i), device_id_type=MESH)

    def send_stats(slots, sends, receives):
        @pl.loop(1, n_dp)
        def _(i):
            stat_copy(slots, sends, receives, i).start()

    st2[md] = forward(split, blocks)
    send_stats(st2, t_s, t_r)

    @pl.when(me > 0)
    def _():
        halo[0].wait_recv()

    @pl.when(me == 0)
    def _():
        pb[:, 0:HALO, :] = jnp.zeros((3, HALO, channels), BF16)
        xt[:, 0:LANES] = jnp.zeros((channels, LANES), BF16)

    widen(HALO - 16, 16)
    product_block(1)
    query_block(1)

    @pl.when(me < n_seq - 1)
    def _():
        halo[2].start()

    @pl.when(me > 0)
    def _():
        halo[1].wait_recv()

    st[md] = forward(0, split)
    send_stats(st, s_s, s_r)

    @pl.loop(0, blocks)
    def _(block):
        here = pl.ds(aligned(block, LANES), LANES)
        for ct in range(cts):
            inn[ct, here, :] = innt[ct * LANES : (ct + 1) * LANES, here].T

    def stack_blocks(g, carry):
        r = pl.ds(aligned(g, MEMBERS), MEMBERS)
        stack = [xt[r, b * LANES : (b + 1) * LANES].astype(F32) for b in range(blocks + 1)]
        stack.append(jnp.zeros((LANES - (blocks + 1) * MEMBERS, LANES), F32))
        xg[g] = jnp.concatenate(stack, axis=0).T.astype(BF16)
        return carry

    lax.fori_loop(0, groups, stack_blocks, 0, unroll=4)

    @pl.when(me > 0)
    def _():
        halo[2].wait_recv()

    widen(0, LANES)
    for ct in range(cts):
        for p in (1, 2):
            kv[(p - 1) * cts + ct, 0:LANES, :] = featured(p, ct, 0)

    token_scale = 1.0 / math.sqrt(rows * n_seq)

    def scales(slots, sends, receives, begin, end):
        @pl.loop(1, n_dp)
        def _(i):
            stat_copy(slots, sends, receives, i, lax.rem(md + i, n_dp)).wait_recv()

        whole = slots[0]
        for i in range(1, n_dp):
            whole = whole + slots[i]
        count = end - begin
        mean = whole * (1.0 / (channels * n_dp))
        rms = jnp.sqrt(mean[0:count] + 1e-05)
        scale_a = token_scale / rms
        scale_b = token_scale * mean[count : 2 * count] / (rms * rms * rms)
        lines_a = [scale_a[b : b + 1] for b in range(count)]
        lines_b = [scale_b[b : b + 1] for b in range(count)]
        for b in range(count):
            at[begin + b] = jnp.broadcast_to(lines_a[b], (LANES, LANES)).T
            bt[begin + b] = jnp.broadcast_to(lines_b[b], (LANES, LANES)).T
        return lines_a, lines_b

    def backward(lines_a, lines_b, begin, end, first):
        pad = jnp.zeros((MEMBERS, LANES), BF16)

        def padded(before, parts):
            after = LANES - before - len(parts) * MEMBERS
            return jnp.concatenate(
                [jnp.zeros((before, LANES), BF16)] * (before > 0) + parts + [jnp.zeros((after, LANES), BF16)],
                axis=0)

        def run(g, carry):
            r = pl.ds(aligned(g, MEMBERS), MEMBERS)
            parts = []
            for b in range(begin, end):
                cols = slice(b * LANES, (b + 1) * LANES)
                parts.append(
                    (ut[r, cols] * lines_a[b - begin] - wt[r, cols] * lines_b[b - begin]).astype(BF16))
            chain = [pad] + parts + [pad]
            left = jnp.concatenate(
                [jnp.concatenate(chain[b : b + 2], axis=1) for b in range(len(chain) - 1)], axis=0)
            grad = dot_nt(left, tob[g])
            for b in range(begin, end + 1):
                cols = slice(b * LANES, (b + 1) * LANES)
                piece = grad[(b - begin) * MEMBERS : (b - begin + 1) * MEMBERS]
                if b == end and not first:
                    piece = piece + pgt[r, cols]
                pgt[r, cols] = piece
            right = jnp.concatenate(
                [padded(begin * MEMBERS, parts), padded((begin + 1) * MEMBERS, parts)], axis=1)
            lagged = dot(xg[g], right)
            square = jnp.where(keep, lagged[:, LANES:], lagged[:, :LANES])
            total = square[0:8]
            for t in range(1, LANES // 8):
                total = total + pltpu.roll(square[8 * t : 8 * t + 8], LANES - 8 * t, 1)
            place = pl.ds(aligned(g, 8), 8)
            bases[place, :] = total if first else bases[place, :] + total
            return carry

        lax.fori_loop(0, groups, run, 0, unroll=8)

    def tail(ct, block, totals, inside):
        cols = slice(ct * LANES, (ct + 1) * LANES)
        gain = sk[ct : ct + 1, :].astype(F32)
        totals = list(totals)
        here = pl.ds(aligned(block, LANES), LANES)
        backed = pgt[cols, here].T
        windows = [
            pf.at[p * cts + ct, pl.ds(aligned(block, LANES), LANES + 16), :] for p in range(3)]
        step = 32

        def taps_of(part, begin, grad):
            for j in range(n_taps):
                term = grad * windows[part][16 - j + begin : 16 - j + begin + step, :]
                totals[part * 8 + j] = totals[part * 8 + j] + fold(term)

        for begin in range(0, LANES, step):
            local = pl.ds(pl.multiple_of(block * LANES + begin, 8), step)
            keys = kv[ct, local, :]
            values = kv[cts + ct, local, :]
            grad = backed[begin : begin + step]
            if inside:
                own = pl.ds(pl.multiple_of((block - 1) * LANES + begin, 16), step)
                queries = qv[ct, own, :]
                inner = inn[ct, own, :]
                first = at[block - 1, begin : begin + step, :]
                second = bt[block - 1, begin : begin + step, :]
                out_grad = cb[own, cols].astype(F32) * first - queries * inner * second
                conv = out_grad * queries
                grad = grad + gain * conv
                product = (keys * values).astype(BF16).astype(F32)
                totals[7] = totals[7] + fold(conv * product)
                taps_of(0, begin, out_grad * inner)
            taps_of(1, begin, grad * values)
            taps_of(2, begin, grad * keys)
        return tuple(totals)

    lines = scales(st2, t_s, t_r, split, blocks)
    backward(*lines, split, blocks, True)
    for ct in range(cts):
        totals = lax.fori_loop(
            split + 1, blocks + 1, lambda block, sums: tail(ct, block, sums, True), (zero8,) * 24)
        for n in range(24):
            tots[ct, n] = totals[n]

    lines = scales(st, s_s, s_r, 0, split)
    backward(*lines, 0, split, False)
    row_all = iota((8 * groups, LANES), 0)
    lag = bases[...]
    for k in (1, 2, 4):
        lag = jnp.where((row_all & k) != 0, pltpu.roll(lag, LANES - k, 1), lag)
    acc[48 : 48 + groups, :] = jnp.concatenate(
        [jnp.sum(lag[8 * g : 8 * g + 8], axis=0, keepdims=True) for g in range(groups)], axis=0)
    for ct in range(cts):
        totals = tail(ct, 0, [tots[ct, n] for n in range(24)], False)
        totals = lax.fori_loop(
            1, split + 1, lambda block, sums: tail(ct, block, sums, True), totals)
        for p in range(3):
            acc[(p * cts + ct) * 8 : (p * cts + ct) * 8 + 8, :] = jnp.concatenate(
                [jnp.sum(totals[p * 8 + j], axis=0, keepdims=True) for j in range(8)], axis=0)

    partner = {"seq": me + 1 - 2 * core}
    swap = pltpu.make_async_remote_copy(
        src_ref=acc.at[pl.ds(aligned(1 - core, half), half), :], dst_ref=slr,
        send_sem=a_s.at[0], recv_sem=a_r.at[0], device_id=partner, device_id_type=MESH)
    swap.start()

    def z_index(i):
        return lax.rem(mz + i, n_z)

    def exchange(slots, sends, receives, place, i, peer):
        return pltpu.make_async_remote_copy(
            src_ref=slots.at[place], dst_ref=slots.at[place], send_sem=sends.at[i],
            recv_sem=receives.at[place], device_id=peer(i), device_id_type=MESH)

    swap.wait_recv()
    sly[my] = (acc[pl.ds(aligned(core, half), half), :] + slr[...]).astype(BF16)

    @pl.loop(1, n_y)
    def _(i):
        exchange(sly, b_s, b_r, my, i, y_peer).start()

    @pl.loop(1, n_y)
    def _(i):
        exchange(sly, b_s, b_r, y_index(i), i, y_peer).wait_recv()

    part = sly[0].astype(F32)
    for i in range(1, n_y):
        part = part + sly[i].astype(F32)
    slz[mz] = part.astype(BF16)

    @pl.loop(1, n_z)
    def _(i):
        exchange(slz, c_s, c_r, mz, i, z_peer).start()

    @pl.loop(1, n_z)
    def _(i):
        exchange(slz, c_s, c_r, z_index(i), i, z_peer).wait_recv()

    for h in range(2):
        part = slz[h].astype(F32)
        for i in range(1, n_z // 2):
            part = part + slz[2 * i + h].astype(F32)
        out[h * half : (h + 1) * half, :] = part

    @pl.loop(1, n_dp)
    def _(i):
        stat_copy(st, s_s, s_r, i).wait_send()
        stat_copy(st2, t_s, t_r, i).wait_send()

    swap.wait_send()

    @pl.loop(1, n_y)
    def _(i):
        exchange(sly, b_s, b_r, my, i, y_peer).wait_send()

    @pl.loop(1, n_z)
    def _(i):
        exchange(slz, c_s, c_r, mz, i, z_peer).wait_send()

    @pl.when(me < n_seq - 1)
    def _():
        for copy in halo:
            copy.wait_send()


def unpack(packed, out_f, out_l, out_s):
    parts, n_taps, channels = out_f.shape
    cts = channels // LANES
    for ct in range(cts):
        cols = slice(ct * LANES, (ct + 1) * LANES)
        for p in range(parts):
            begin = (p * cts + ct) * 8
            out_f[p, :, cols] = packed[begin : begin + n_taps, :]
        out_s[:, cols] = packed[ct * 8 + 7 : ct * 8 + 8, :]
    out_l[...] = packed[parts * cts * 8 :, :]


def body(sizes, projected, featurizer, long_filter, skip_gain, out_cotangent):
    n_seq, n_dp = sizes
    parts, rows, channels = projected.shape
    n_taps = featurizer.shape[0]
    groups, filter_taps = long_filter.shape
    n_y = 1 << ((n_seq.bit_length() - 1) // 2)
    n_z = n_seq // n_y
    blocks = rows // LANES
    cts = channels // LANES
    geo = (n_seq, n_dp, n_y, n_z, rows, n_taps, channels)
    long = rows + LANES
    vmem = pltpu.VMEM
    dma = pltpu.SemaphoreType.DMA
    scratch = [
        vmem((3, HALO + rows, channels), BF16),
        vmem((rows, channels), BF16),
        vmem((3, n_taps, channels), BF16),
        vmem((groups, LANES), BF16),
        vmem((cts, LANES), BF16),
        vmem((groups, LANES), F32),
        vmem((3, 8, channels), F32),
        vmem((3 * cts, HALO + rows, LANES), F32),
        vmem((2 * cts, long, LANES), F32),
        vmem((cts, rows, LANES), F32),
        vmem((channels, long), BF16),
        vmem((channels, rows), F32),
        vmem((channels, rows), F32),
        vmem((channels, rows), F32),
        vmem((channels, rows), F32),
        vmem((channels, rows), F32),
        vmem((cts, rows, LANES), F32),
        vmem((groups, 2 * LANES, LANES), BF16),
        vmem((groups, LANES, 2 * LANES), BF16),
        vmem((groups, LANES, LANES), BF16),
        vmem((channels, long), F32),
        vmem((channels, LANES), F32),
        vmem((blocks, LANES, LANES), F32),
        vmem((blocks, LANES, LANES), F32),
        vmem((n_dp, blocks // 2 * 2, LANES), F32),
        vmem((n_dp, blocks // 2 * 2, LANES), F32),
        vmem((64, LANES), F32),
        vmem((cts, 24, 8, LANES), F32),
        vmem((8 * groups, LANES), F32),
        vmem((32, LANES), F32),
        vmem((n_y, 32, LANES), BF16),
        vmem((n_z, 32, LANES), BF16),
        dma((5,)), dma((3,)), dma((3,)),
        dma((n_dp,)), dma((n_dp,)),
        dma((n_dp,)), dma((n_dp,)),
        dma((1,)), dma((1,)),
        dma((n_y,)), dma((n_y,)),
        dma((n_z,)), dma((n_z,)),
    ]
    inside = pl.BlockSpec(memory_space=pltpu.VMEM)
    packed = pl.pallas_call(
        functools.partial(kernel, geo),
        out_shape=jax.ShapeDtypeStruct((64, LANES), F32),
        in_specs=[pl.BlockSpec(memory_space=pltpu.HBM)] * 5,
        out_specs=inside,
        scratch_shapes=scratch,
        compiler_params=pltpu.CompilerParams(
            collective_id=0, has_side_effects=True, vmem_limit_bytes=60 * 1024 * 1024),
    )(projected, featurizer.transpose(1, 0, 2), long_filter, skip_gain.reshape(cts, LANES), out_cotangent)
    feat, filt, skip = pl.pallas_call(
        unpack,
        out_shape=(
            jax.ShapeDtypeStruct((parts, n_taps, channels), F32),
            jax.ShapeDtypeStruct((groups, filter_taps), F32),
            jax.ShapeDtypeStruct((1, channels), F32),
        ),
        in_specs=[inside],
        out_specs=(inside,) * 3,
        compiler_params=pltpu.CompilerParams(vmem_limit_bytes=60 * 1024 * 1024),
    )(packed)
    return feat.transpose(1, 0, 2), filt, skip.reshape(channels)


def solution(mesh):
    sizes = (mesh.shape["seq"], mesh.shape["dp"])
    return jax.shard_map(
        functools.partial(body, sizes),
        mesh=mesh,
        in_specs=(
            P(None, "seq", "dp"),
            P(None, None, "dp"),
            P("dp", None),
            P("dp"),
            P("seq", "dp"),
        ),
        out_specs=(P(None, None, "dp"), P("dp", None), P("dp")),
        check_vma=False,
    )
```

```python
import functools
import math

import jax
import jax.numpy as jnp
from jax import lax
from jax.experimental import pallas as pl
from jax.experimental.pallas import tpu as pltpu
from jax.sharding import PartitionSpec as P

F32 = jnp.float32
BF16 = jnp.bfloat16
LANES = 128
MEMBERS = 16
HALO = 144
MESH = pl.DeviceIdType.MESH


def iota(shape, dim):
    return lax.broadcasted_iota(jnp.int32, shape, dim)


def dot(lhs, rhs):
    return lax.dot_general(lhs, rhs, (((1,), (0,)), ((), ())), preferred_element_type=F32)


def dot_nt(lhs, rhs):
    return lax.dot_general(lhs, rhs, (((1,), (1,)), ((), ())), preferred_element_type=F32)


def aligned(index, step):
    return pl.multiple_of(index * step, step)


def fold(array):
    total = array[0:8]
    for begin in range(8, array.shape[0], 8):
        total = total + array[begin : begin + 8]
    return total


def kernel(geo, proj, taps, filt, skip, cot, out,
           pb, cb, tr, lf, sk, lff, wv, pf, kv, qv, xt, qt, gt, innt, ut, wt, inn, tof, tob, xg,
           pgt, skt, at, bt, st, st2, acc, tots, bases, slr, sly, slz,
           ld_sem, h_s, h_r, s_s, s_r, t_s, t_r, a_s, a_r, b_s, b_r, c_s, c_r):
    n_seq, n_dp, n_y, n_z, rows, n_taps, channels = geo
    blocks = rows // LANES
    groups = channels // MEMBERS
    cts = channels // LANES
    me = lax.axis_index("seq")
    md = lax.axis_index("dp")
    my = me // n_z
    mz = lax.rem(me, n_z)
    core = lax.rem(mz, 2)
    half = 32

    loads = [
        pltpu.make_async_copy(filt, lf, ld_sem.at[0]),
        pltpu.make_async_copy(taps, tr, ld_sem.at[1]),
        pltpu.make_async_copy(skip, sk, ld_sem.at[2]),
        pltpu.make_async_copy(
            proj.at[pl.ds(1, 2), pl.ds(rows - HALO, HALO), :],
            pb.at[pl.ds(1, 2), pl.ds(rows, HALO), :], ld_sem.at[3]),
        pltpu.make_async_copy(cot, cb, ld_sem.at[4]),
        pltpu.make_async_copy(
            proj.at[pl.ds(1, 2), pl.ds(0, rows - HALO), :],
            pb.at[pl.ds(1, 2), pl.ds(HALO, rows - HALO), :], ld_sem.at[5]),
        pltpu.make_async_copy(
            proj.at[pl.ds(0, 1), :, :], pb.at[pl.ds(0, 1), pl.ds(HALO, rows), :], ld_sem.at[6]),
    ]
    barrier = pltpu.get_barrier_semaphore()

    def dp_peer(i):
        return {"dp": lax.rem(md + i, n_dp)}

    def y_index(i):
        return lax.rem(my + i, n_y)

    def y_peer(i):
        return {"seq": y_index(i) * n_z + mz}

    def z_peer(i):
        return {"seq": my * n_z + lax.rem(mz + i, n_z)}

    def greet(peer, count):
        @pl.loop(1, count)
        def _(i):
            pl.semaphore_signal(barrier, 1, device_id=peer(i), device_id_type=MESH)

    ahead = {"seq": lax.rem(me + 1, n_seq)}
    behind = {"seq": lax.rem(me + n_seq - 1, n_seq)}
    pl.semaphore_signal(barrier, 1, device_id=behind, device_id_type=MESH)
    pl.semaphore_signal(barrier, 1, device_id=ahead, device_id_type=MESH)
    for copy in loads:
        copy.start()
    greet(dp_peer, n_dp)
    greet(y_peer, n_y)
    greet(z_peer, n_z)

    for copy in loads[:3]:
        copy.wait()
    for p in range(3):
        wv[p, 0:n_taps, :] = tr[p].astype(F32)

    def featured(p, ct, block):
        window = pf.at[p * cts + ct, pl.ds(aligned(block, LANES), LANES + 16), :]
        total = None
        for j in range(n_taps):
            term = wv[p, j : j + 1, ct * LANES : (ct + 1) * LANES] * window[16 - j : 16 - j + LANES, :]
            total = term if total is None else total + term
        return total.astype(BF16).astype(F32)

    def widen(begin, count, parts=(0, 1, 2)):
        for p in parts:
            for ct in range(cts):
                pf[p * cts + ct, pl.ds(begin, count), :] = pb[
                    p, pl.ds(begin, count), ct * LANES : (ct + 1) * LANES].astype(F32)

    def product_block(block):
        for ct in range(cts):
            cols = slice(ct * LANES, (ct + 1) * LANES)
            here = pl.ds(aligned(block, LANES), LANES)
            keys = featured(1, ct, block)
            values = featured(2, ct, block)
            kv[ct, here, :] = keys
            kv[cts + ct, here, :] = values
            product = (keys * values).astype(BF16)
            xt[cols, here] = product.astype(F32).T.astype(BF16)

    def query_block(block):
        for ct in range(cts):
            cols = slice(ct * LANES, (ct + 1) * LANES)
            inside = pl.ds(aligned(block - 1, LANES), LANES)
            queries = featured(0, ct, block)
            qv[ct, inside, :] = queries
            qt[cols, inside] = queries.T
            gt[cols, inside] = cb[inside, cols].astype(F32).T

    loads[3].wait()

    widen(rows, HALO, (1, 2))
    product_block(blocks)

    pl.semaphore_wait(barrier, n_dp + n_y + n_z - 1)

    def rim(number, src, dst):
        return pltpu.make_async_remote_copy(
            src_ref=src, dst_ref=dst, send_sem=h_s.at[number], recv_sem=h_r.at[number],
            device_id=ahead, device_id_type=MESH)

    halo = [
        rim(0, proj.at[:, pl.ds(rows - 16, 16), :], pb.at[:, pl.ds(HALO - 16, 16), :]),
        rim(1, xt.at[:, pl.ds(rows, LANES)], xt.at[:, pl.ds(0, LANES)]),
        rim(2, proj.at[pl.ds(1, 2), pl.ds(rows - HALO, LANES), :],
            pb.at[pl.ds(1, 2), pl.ds(0, LANES), :]),
    ]

    @pl.when(me < n_seq - 1)
    def _():
        halo[0].start()
        halo[1].start()

    for copy in loads[4:]:
        copy.wait()
    widen(HALO, rows - HALO, (1, 2))
    widen(HALO, rows, (0,))

    @pl.loop(2, blocks)
    def _(block):
        product_block(block)

    @pl.loop(2, blocks + 1)
    def _(block):
        query_block(block)

    lff[...] = lf[...].astype(F32)
    row_all = iota((8 * groups, LANES), 0)
    keep = iota((LANES, LANES), 1) >= iota((LANES, LANES), 0)
    base = jnp.concatenate(
        [jnp.broadcast_to(lff[g : g + 1, :], (8, LANES)) for g in range(groups)], axis=0)
    for k in (1, 2, 4):
        base = jnp.where((row_all & k) != 0, pltpu.roll(base, k, 1), base)
    bases[...] = base

    def toeplitz(g, carry):
        base = bases[pl.ds(aligned(g, 8), 8), :]
        tiles = [base] + [pltpu.roll(base, 8 * r, 1) for r in range(1, LANES // 8)]
        circ = jnp.concatenate(tiles, axis=0)
        near = jnp.where(keep, circ, 0.0).astype(BF16)
        far = jnp.where(keep, 0.0, circ).astype(BF16)
        tof[g, 0:LANES, :] = far
        tof[g, LANES : 2 * LANES, :] = near
        tob[g, :, 0:LANES] = near
        tob[g, :, LANES : 2 * LANES] = far
        return carry

    lax.fori_loop(0, groups, toeplitz, 0, unroll=4)

    for ct in range(cts):
        cols = slice(ct * LANES, (ct + 1) * LANES)
        line = jnp.broadcast_to(sk[ct : ct + 1, :].astype(F32), (LANES, LANES))
        skt[cols, :] = line.T

    zero8 = jnp.zeros((8, LANES), F32)
    split = blocks // 2

    def forward(begin, end):
        def run(g, sums):
            sums = list(sums)
            r = pl.ds(aligned(g, MEMBERS), MEMBERS)
            source = [xt[r, b * LANES : (b + 1) * LANES] for b in range(begin, end + 1)]
            left = jnp.concatenate(
                [jnp.concatenate(source[b : b + 2], axis=1) for b in range(end - begin)], axis=0)
            filtered = dot(left, tof[g])
            gain = skt[r, :]
            for b in range(end - begin):
                cols = slice((begin + b) * LANES, (begin + b + 1) * LANES)
                inner = filtered[b * MEMBERS : (b + 1) * MEMBERS] + gain * source[b + 1].astype(F32)
                queries = qt[r, cols]
                output = queries * inner
                cotangent = gt[r, cols]
                sums[b] = sums[b] + fold(output * output)
                sums[end - begin + b] = sums[end - begin + b] + fold(cotangent * output)
                innt[r, cols] = inner
                ut[r, cols] = cotangent * queries
                wt[r, cols] = output * queries
            return tuple(sums)

        sums = lax.fori_loop(0, groups, run, (zero8,) * (2 * (end - begin)), unroll=8)
        return jnp.concatenate([jnp.sum(part, axis=0, keepdims=True) for part in sums], axis=0)

    def stat_copy(slots, sends, receives, i, index=None):
        place = md if index is None else index
        return pltpu.make_async_remote_copy(
            src_ref=slots.at[place], dst_ref=slots.at[place], send_sem=sends.at[i],
            recv_sem=receives.at[place], device_id=dp_peer(i), device_id_type=MESH)

    def send_stats(slots, sends, receives):
        @pl.loop(1, n_dp)
        def _(i):
            stat_copy(slots, sends, receives, i).start()

    st2[md] = forward(split, blocks)
    send_stats(st2, t_s, t_r)

    @pl.when(me > 0)
    def _():
        halo[0].wait_recv()

    @pl.when(me == 0)
    def _():
        pb[:, 0:HALO, :] = jnp.zeros((3, HALO, channels), BF16)
        xt[:, 0:LANES] = jnp.zeros((channels, LANES), BF16)

    widen(HALO - 16, 16)
    product_block(1)
    query_block(1)

    @pl.when(me < n_seq - 1)
    def _():
        halo[2].start()

    @pl.when(me > 0)
    def _():
        halo[1].wait_recv()

    st[md] = forward(0, split)
    send_stats(st, s_s, s_r)

    @pl.loop(0, blocks)
    def _(block):
        here = pl.ds(aligned(block, LANES), LANES)
        for ct in range(cts):
            inn[ct, here, :] = innt[ct * LANES : (ct + 1) * LANES, here].T

    def stack_blocks(g, carry):
        r = pl.ds(aligned(g, MEMBERS), MEMBERS)
        stack = [xt[r, b * LANES : (b + 1) * LANES].astype(F32) for b in range(blocks + 1)]
        stack.append(jnp.zeros((LANES - (blocks + 1) * MEMBERS, LANES), F32))
        xg[g] = jnp.concatenate(stack, axis=0).T.astype(BF16)
        return carry

    lax.fori_loop(0, groups, stack_blocks, 0, unroll=4)

    @pl.when(me > 0)
    def _():
        halo[2].wait_recv()

    widen(0, LANES)
    for ct in range(cts):
        for p in (1, 2):
            kv[(p - 1) * cts + ct, 0:LANES, :] = featured(p, ct, 0)

    token_scale = 1.0 / math.sqrt(rows * n_seq)

    def scales(slots, sends, receives, begin, end):
        @pl.loop(1, n_dp)
        def _(i):
            stat_copy(slots, sends, receives, i, lax.rem(md + i, n_dp)).wait_recv()

        whole = slots[0]
        for i in range(1, n_dp):
            whole = whole + slots[i]
        count = end - begin
        mean = whole * (1.0 / (channels * n_dp))
        rms = jnp.sqrt(mean[0:count] + 1e-05)
        scale_a = token_scale / rms
        scale_b = token_scale * mean[count : 2 * count] / (rms * rms * rms)
        lines_a = [scale_a[b : b + 1] for b in range(count)]
        lines_b = [scale_b[b : b + 1] for b in range(count)]
        for b in range(count):
            at[begin + b] = jnp.broadcast_to(lines_a[b], (LANES, LANES)).T
            bt[begin + b] = jnp.broadcast_to(lines_b[b], (LANES, LANES)).T
        return lines_a, lines_b

    def backward(lines_a, lines_b, begin, end, first):
        pad = jnp.zeros((MEMBERS, LANES), BF16)

        def padded(before, parts):
            after = LANES - before - len(parts) * MEMBERS
            return jnp.concatenate(
                [jnp.zeros((before, LANES), BF16)] * (before > 0) + parts + [jnp.zeros((after, LANES), BF16)],
                axis=0)

        def run(g, carry):
            r = pl.ds(aligned(g, MEMBERS), MEMBERS)
            parts = []
            for b in range(begin, end):
                cols = slice(b * LANES, (b + 1) * LANES)
                parts.append(
                    (ut[r, cols] * lines_a[b - begin] - wt[r, cols] * lines_b[b - begin]).astype(BF16))
            chain = [pad] + parts + [pad]
            left = jnp.concatenate(
                [jnp.concatenate(chain[b : b + 2], axis=1) for b in range(len(chain) - 1)], axis=0)
            grad = dot_nt(left, tob[g])
            for b in range(begin, end + 1):
                cols = slice(b * LANES, (b + 1) * LANES)
                piece = grad[(b - begin) * MEMBERS : (b - begin + 1) * MEMBERS]
                if b == end and not first:
                    piece = piece + pgt[r, cols]
                pgt[r, cols] = piece
            right = jnp.concatenate(
                [padded(begin * MEMBERS, parts), padded((begin + 1) * MEMBERS, parts)], axis=1)
            lagged = dot(xg[g], right)
            square = jnp.where(keep, lagged[:, LANES:], lagged[:, :LANES])
            total = square[0:8]
            for t in range(1, LANES // 8):
                total = total + pltpu.roll(square[8 * t : 8 * t + 8], LANES - 8 * t, 1)
            place = pl.ds(aligned(g, 8), 8)
            bases[place, :] = total if first else bases[place, :] + total
            return carry

        lax.fori_loop(0, groups, run, 0, unroll=8)

    def tail(ct, block, totals, inside):
        cols = slice(ct * LANES, (ct + 1) * LANES)
        gain = sk[ct : ct + 1, :].astype(F32)
        totals = list(totals)
        here = pl.ds(aligned(block, LANES), LANES)
        backed = pgt[cols, here].T
        windows = [
            pf.at[p * cts + ct, pl.ds(aligned(block, LANES), LANES + 16), :] for p in range(3)]
        step = 32

        def taps_of(part, begin, grad):
            for j in range(n_taps):
                term = grad * windows[part][16 - j + begin : 16 - j + begin + step, :]
                totals[part * 8 + j] = totals[part * 8 + j] + fold(term)

        for begin in range(0, LANES, step):
            local = pl.ds(pl.multiple_of(block * LANES + begin, 8), step)
            keys = kv[ct, local, :]
            values = kv[cts + ct, local, :]
            grad = backed[begin : begin + step]
            if inside:
                own = pl.ds(pl.multiple_of((block - 1) * LANES + begin, 16), step)
                queries = qv[ct, own, :]
                inner = inn[ct, own, :]
                first = at[block - 1, begin : begin + step, :]
                second = bt[block - 1, begin : begin + step, :]
                out_grad = cb[own, cols].astype(F32) * first - queries * inner * second
                conv = out_grad * queries
                grad = grad + gain * conv
                product = (keys * values).astype(BF16).astype(F32)
                totals[7] = totals[7] + fold(conv * product)
                taps_of(0, begin, out_grad * inner)
            taps_of(1, begin, grad * values)
            taps_of(2, begin, grad * keys)
        return tuple(totals)

    lines = scales(st2, t_s, t_r, split, blocks)
    backward(*lines, split, blocks, True)
    for ct in range(cts):
        totals = lax.fori_loop(
            split + 1, blocks + 1, lambda block, sums: tail(ct, block, sums, True), (zero8,) * 24)
        for n in range(24):
            tots[ct, n] = totals[n]

    lines = scales(st, s_s, s_r, 0, split)
    backward(*lines, 0, split, False)
    row_all = iota((8 * groups, LANES), 0)
    lag = bases[...]
    for k in (1, 2, 4):
        lag = jnp.where((row_all & k) != 0, pltpu.roll(lag, LANES - k, 1), lag)
    acc[48 : 48 + groups, :] = jnp.concatenate(
        [jnp.sum(lag[8 * g : 8 * g + 8], axis=0, keepdims=True) for g in range(groups)], axis=0)
    for ct in range(cts):
        totals = tail(ct, 0, [tots[ct, n] for n in range(24)], False)
        totals = lax.fori_loop(
            1, split + 1, lambda block, sums: tail(ct, block, sums, True), totals)
        for p in range(3):
            acc[(p * cts + ct) * 8 : (p * cts + ct) * 8 + 8, :] = jnp.concatenate(
                [jnp.sum(totals[p * 8 + j], axis=0, keepdims=True) for j in range(8)], axis=0)

    partner = {"seq": me + 1 - 2 * core}
    swap = pltpu.make_async_remote_copy(
        src_ref=acc.at[pl.ds(aligned(1 - core, half), half), :], dst_ref=slr,
        send_sem=a_s.at[0], recv_sem=a_r.at[0], device_id=partner, device_id_type=MESH)
    swap.start()

    def z_index(i):
        return lax.rem(mz + i, n_z)

    def exchange(slots, sends, receives, place, i, peer):
        return pltpu.make_async_remote_copy(
            src_ref=slots.at[place], dst_ref=slots.at[place], send_sem=sends.at[i],
            recv_sem=receives.at[place], device_id=peer(i), device_id_type=MESH)

    swap.wait_recv()
    sly[my] = (acc[pl.ds(aligned(core, half), half), :] + slr[...]).astype(BF16)

    @pl.loop(1, n_y)
    def _(i):
        exchange(sly, b_s, b_r, my, i, y_peer).start()

    @pl.loop(1, n_y)
    def _(i):
        exchange(sly, b_s, b_r, y_index(i), i, y_peer).wait_recv()

    part = sly[0].astype(F32)
    for i in range(1, n_y):
        part = part + sly[i].astype(F32)
    slz[mz] = part.astype(BF16)

    @pl.loop(1, n_z)
    def _(i):
        exchange(slz, c_s, c_r, mz, i, z_peer).start()

    @pl.loop(1, n_z)
    def _(i):
        exchange(slz, c_s, c_r, z_index(i), i, z_peer).wait_recv()

    for h in range(2):
        part = slz[h].astype(F32)
        for i in range(1, n_z // 2):
            part = part + slz[2 * i + h].astype(F32)
        out[h * half : (h + 1) * half, :] = part

    @pl.loop(1, n_dp)
    def _(i):
        stat_copy(st, s_s, s_r, i).wait_send()
        stat_copy(st2, t_s, t_r, i).wait_send()

    swap.wait_send()

    @pl.loop(1, n_y)
    def _(i):
        exchange(sly, b_s, b_r, my, i, y_peer).wait_send()

    @pl.loop(1, n_z)
    def _(i):
        exchange(slz, c_s, c_r, mz, i, z_peer).wait_send()

    @pl.when(me < n_seq - 1)
    def _():
        for copy in halo:
            copy.wait_send()


def unpack(packed, out_f, out_l, out_s):
    parts, n_taps, channels = out_f.shape
    cts = channels // LANES
    for ct in range(cts):
        cols = slice(ct * LANES, (ct + 1) * LANES)
        for p in range(parts):
            begin = (p * cts + ct) * 8
            out_f[p, :, cols] = packed[begin : begin + n_taps, :]
        out_s[:, cols] = packed[ct * 8 + 7 : ct * 8 + 8, :]
    out_l[...] = packed[parts * cts * 8 :, :]


def body(sizes, projected, featurizer, long_filter, skip_gain, out_cotangent):
    n_seq, n_dp = sizes
    parts, rows, channels = projected.shape
    n_taps = featurizer.shape[0]
    groups, filter_taps = long_filter.shape
    n_y = 1 << ((n_seq.bit_length() - 1) // 2)
    n_z = n_seq // n_y
    blocks = rows // LANES
    cts = channels // LANES
    geo = (n_seq, n_dp, n_y, n_z, rows, n_taps, channels)
    long = rows + LANES
    vmem = pltpu.VMEM
    dma = pltpu.SemaphoreType.DMA
    scratch = [
        vmem((3, HALO + rows, channels), BF16),
        vmem((rows, channels), BF16),
        vmem((3, n_taps, channels), BF16),
        vmem((groups, LANES), BF16),
        vmem((cts, LANES), BF16),
        vmem((groups, LANES), F32),
        vmem((3, 8, channels), F32),
        vmem((3 * cts, HALO + rows, LANES), F32),
        vmem((2 * cts, long, LANES), F32),
        vmem((cts, rows, LANES), F32),
        vmem((channels, long), BF16),
        vmem((channels, rows), F32),
        vmem((channels, rows), F32),
        vmem((channels, rows), F32),
        vmem((channels, rows), F32),
        vmem((channels, rows), F32),
        vmem((cts, rows, LANES), F32),
        vmem((groups, 2 * LANES, LANES), BF16),
        vmem((groups, LANES, 2 * LANES), BF16),
        vmem((groups, LANES, LANES), BF16),
        vmem((channels, long), F32),
        vmem((channels, LANES), F32),
        vmem((blocks, LANES, LANES), F32),
        vmem((blocks, LANES, LANES), F32),
        vmem((n_dp, blocks // 2 * 2, LANES), F32),
        vmem((n_dp, blocks // 2 * 2, LANES), F32),
        vmem((64, LANES), F32),
        vmem((cts, 24, 8, LANES), F32),
        vmem((8 * groups, LANES), F32),
        vmem((32, LANES), F32),
        vmem((n_y, 32, LANES), BF16),
        vmem((n_z, 32, LANES), BF16),
        dma((7,)), dma((3,)), dma((3,)),
        dma((n_dp,)), dma((n_dp,)),
        dma((n_dp,)), dma((n_dp,)),
        dma((1,)), dma((1,)),
        dma((n_y,)), dma((n_y,)),
        dma((n_z,)), dma((n_z,)),
    ]
    inside = pl.BlockSpec(memory_space=pltpu.VMEM)
    packed = pl.pallas_call(
        functools.partial(kernel, geo),
        out_shape=jax.ShapeDtypeStruct((64, LANES), F32),
        in_specs=[pl.BlockSpec(memory_space=pltpu.HBM)] * 5,
        out_specs=inside,
        scratch_shapes=scratch,
        compiler_params=pltpu.CompilerParams(
            collective_id=0, has_side_effects=True, vmem_limit_bytes=60 * 1024 * 1024),
    )(projected, featurizer.transpose(1, 0, 2), long_filter, skip_gain.reshape(cts, LANES), out_cotangent)
    feat, filt, skip = pl.pallas_call(
        unpack,
        out_shape=(
            jax.ShapeDtypeStruct((parts, n_taps, channels), F32),
            jax.ShapeDtypeStruct((groups, filter_taps), F32),
            jax.ShapeDtypeStruct((1, channels), F32),
        ),
        in_specs=[inside],
        out_specs=(inside,) * 3,
        compiler_params=pltpu.CompilerParams(vmem_limit_bytes=60 * 1024 * 1024),
    )(packed)
    return feat.transpose(1, 0, 2), filt, skip.reshape(channels)


def solution(mesh):
    sizes = (mesh.shape["seq"], mesh.shape["dp"])
    return jax.shard_map(
        functools.partial(body, sizes),
        mesh=mesh,
        in_specs=(
            P(None, "seq", "dp"),
            P(None, None, "dp"),
            P("dp", None),
            P("dp"),
            P("seq", "dp"),
        ),
        out_specs=(P(None, None, "dp"), P("dp", None), P("dp")),
        check_vma=False,
    )
```

```python
import functools
import math

import jax
import jax.numpy as jnp
from jax import lax
from jax.experimental import pallas as pl
from jax.experimental.pallas import tpu as pltpu
from jax.sharding import PartitionSpec as P

F32 = jnp.float32
BF16 = jnp.bfloat16
LANES = 128
MEMBERS = 16
HALO = 144
MESH = pl.DeviceIdType.MESH


def iota(shape, dim):
    return lax.broadcasted_iota(jnp.int32, shape, dim)


def dot(lhs, rhs):
    return lax.dot_general(lhs, rhs, (((1,), (0,)), ((), ())), preferred_element_type=F32)


def dot_nt(lhs, rhs):
    return lax.dot_general(lhs, rhs, (((1,), (1,)), ((), ())), preferred_element_type=F32)


def aligned(index, step):
    return pl.multiple_of(index * step, step)


def far_first(count, ring, step):
    def distance(i):
        return min(i % ring, ring - i % ring) // step

    return sorted(range(1, count), key=distance, reverse=True)


def fold(array):
    total = array[0:8]
    for begin in range(8, array.shape[0], 8):
        total = total + array[begin : begin + 8]
    return total


def kernel(geo, proj, taps, filt, skip, cot, out,
           pb, cb, tr, lf, sk, lff, wv, pf, kv, qv, xt, qt, gt, innt, ut, wt, inn, tof, tob, xg,
           pgt, skt, at, bt, st, st2, acc, tots, bases, slr, sly, slz,
           ld_sem, h_s, h_r, s_s, s_r, t_s, t_r, a_s, a_r, b_s, b_r, c_s, c_r):
    n_seq, n_dp, n_y, n_z, rows, n_taps, channels = geo
    blocks = rows // LANES
    groups = channels // MEMBERS
    cts = channels // LANES
    me = lax.axis_index("seq")
    md = lax.axis_index("dp")
    my = me // n_z
    mz = lax.rem(me, n_z)
    core = lax.rem(mz, 2)
    half = 32

    loads = [
        pltpu.make_async_copy(filt, lf, ld_sem.at[0]),
        pltpu.make_async_copy(taps, tr, ld_sem.at[1]),
        pltpu.make_async_copy(skip, sk, ld_sem.at[2]),
        pltpu.make_async_copy(proj, pb.at[:, pl.ds(HALO, rows), :], ld_sem.at[3]),
        pltpu.make_async_copy(cot, cb, ld_sem.at[4]),
    ]
    barrier = pltpu.get_barrier_semaphore()

    def dp_peer(i):
        return {"dp": lax.rem(md + i, n_dp)}

    def y_index(i):
        return lax.rem(my + i, n_y)

    def y_peer(i):
        return {"seq": y_index(i) * n_z + mz}

    def z_peer(i):
        return {"seq": my * n_z + lax.rem(mz + i, n_z)}

    def greet(peer, count):
        @pl.loop(1, count)
        def _(i):
            pl.semaphore_signal(barrier, 1, device_id=peer(i), device_id_type=MESH)

    ahead = {"seq": lax.rem(me + 1, n_seq)}
    behind = {"seq": lax.rem(me + n_seq - 1, n_seq)}
    pl.semaphore_signal(barrier, 1, device_id=behind, device_id_type=MESH)
    pl.semaphore_signal(barrier, 1, device_id=ahead, device_id_type=MESH)
    for copy in loads:
        copy.start()
    greet(dp_peer, n_dp)
    greet(y_peer, n_y)
    greet(z_peer, n_z)

    for copy in loads[:3]:
        copy.wait()
    for p in range(3):
        wv[p, 0:n_taps, :] = tr[p].astype(F32)

    def featured(p, ct, block):
        window = pf.at[p * cts + ct, pl.ds(aligned(block, LANES), LANES + 16), :]
        total = None
        for j in range(n_taps):
            term = wv[p, j : j + 1, ct * LANES : (ct + 1) * LANES] * window[16 - j : 16 - j + LANES, :]
            total = term if total is None else total + term
        return total.astype(BF16).astype(F32)

    def widen(begin, count):
        for p in range(3):
            for ct in range(cts):
                pf[p * cts + ct, pl.ds(begin, count), :] = pb[
                    p, pl.ds(begin, count), ct * LANES : (ct + 1) * LANES].astype(F32)

    def product_block(block):
        for ct in range(cts):
            cols = slice(ct * LANES, (ct + 1) * LANES)
            here = pl.ds(aligned(block, LANES), LANES)
            keys = featured(1, ct, block)
            values = featured(2, ct, block)
            kv[ct, here, :] = keys
            kv[cts + ct, here, :] = values
            product = (keys * values).astype(BF16)
            xt[cols, here] = product.astype(F32).T.astype(BF16)

    def query_block(block):
        for ct in range(cts):
            cols = slice(ct * LANES, (ct + 1) * LANES)
            inside = pl.ds(aligned(block - 1, LANES), LANES)
            queries = featured(0, ct, block)
            qv[ct, inside, :] = queries
            qt[cols, inside] = queries.T
            gt[cols, inside] = cb[inside, cols].astype(F32).T

    loads[3].wait()

    @pl.loop(0, blocks)
    def _(block):
        widen(pl.multiple_of(HALO + block * LANES, 16), LANES)

    product_block(blocks)

    pl.semaphore_wait(barrier, n_dp + n_y + n_z - 1)

    def rim(number, src, dst):
        return pltpu.make_async_remote_copy(
            src_ref=src, dst_ref=dst, send_sem=h_s.at[number], recv_sem=h_r.at[number],
            device_id=ahead, device_id_type=MESH)

    halo = [
        rim(0, proj.at[:, pl.ds(rows - 16, 16), :], pb.at[:, pl.ds(HALO - 16, 16), :]),
        rim(1, xt.at[:, pl.ds(rows, LANES)], xt.at[:, pl.ds(0, LANES)]),
        rim(2, proj.at[pl.ds(1, 2), pl.ds(rows - HALO, LANES), :],
            pb.at[pl.ds(1, 2), pl.ds(0, LANES), :]),
    ]

    @pl.when(me < n_seq - 1)
    def _():
        halo[0].start()
        halo[1].start()

    loads[4].wait()

    @pl.loop(2, blocks)
    def _(block):
        product_block(block)

    @pl.loop(2, blocks + 1)
    def _(block):
        query_block(block)

    lff[...] = lf[...].astype(F32)
    row_all = iota((8 * groups, LANES), 0)
    keep = iota((LANES, LANES), 1) >= iota((LANES, LANES), 0)
    base = jnp.concatenate(
        [jnp.broadcast_to(lff[g : g + 1, :], (8, LANES)) for g in range(groups)], axis=0)
    for k in (1, 2, 4):
        base = jnp.where((row_all & k) != 0, pltpu.roll(base, k, 1), base)
    bases[...] = base

    def toeplitz(g, carry):
        base = bases[pl.ds(aligned(g, 8), 8), :]
        tiles = [base] + [pltpu.roll(base, 8 * r, 1) for r in range(1, LANES // 8)]
        circ = jnp.concatenate(tiles, axis=0)
        near = jnp.where(keep, circ, 0.0).astype(BF16)
        far = jnp.where(keep, 0.0, circ).astype(BF16)
        tof[g, 0:LANES, :] = far
        tof[g, LANES : 2 * LANES, :] = near
        tob[g, :, 0:LANES] = near
        tob[g, :, LANES : 2 * LANES] = far
        return carry

    lax.fori_loop(0, groups, toeplitz, 0, unroll=4)

    for ct in range(cts):
        cols = slice(ct * LANES, (ct + 1) * LANES)
        line = jnp.broadcast_to(sk[ct : ct + 1, :].astype(F32), (LANES, LANES))
        skt[cols, :] = line.T

    zero8 = jnp.zeros((8, LANES), F32)
    split = blocks // 2

    def forward(begin, end):
        def run(g, sums):
            sums = list(sums)
            r = pl.ds(aligned(g, MEMBERS), MEMBERS)
            source = [xt[r, b * LANES : (b + 1) * LANES] for b in range(begin, end + 1)]
            left = jnp.concatenate(
                [jnp.concatenate(source[b : b + 2], axis=1) for b in range(end - begin)], axis=0)
            filtered = dot(left, tof[g])
            gain = skt[r, :]
            for b in range(end - begin):
                cols = slice((begin + b) * LANES, (begin + b + 1) * LANES)
                inner = filtered[b * MEMBERS : (b + 1) * MEMBERS] + gain * source[b + 1].astype(F32)
                queries = qt[r, cols]
                output = queries * inner
                cotangent = gt[r, cols]
                sums[b] = sums[b] + fold(output * output)
                sums[end - begin + b] = sums[end - begin + b] + fold(cotangent * output)
                innt[r, cols] = inner
                ut[r, cols] = cotangent * queries
                wt[r, cols] = output * queries
            return tuple(sums)

        sums = lax.fori_loop(0, groups, run, (zero8,) * (2 * (end - begin)), unroll=8)
        return jnp.concatenate([jnp.sum(part, axis=0, keepdims=True) for part in sums], axis=0)

    def stat_copy(slots, sends, receives, i, index=None):
        place = md if index is None else index
        return pltpu.make_async_remote_copy(
            src_ref=slots.at[place], dst_ref=slots.at[place], send_sem=sends.at[i],
            recv_sem=receives.at[place], device_id=dp_peer(i), device_id_type=MESH)

    def send_stats(slots, sends, receives):
        for i in far_first(n_dp, n_dp // 2, 1):
            stat_copy(slots, sends, receives, i).start()

    st2[md] = forward(split, blocks)
    send_stats(st2, t_s, t_r)

    @pl.when(me > 0)
    def _():
        halo[0].wait_recv()

    @pl.when(me == 0)
    def _():
        pb[:, 0:HALO, :] = jnp.zeros((3, HALO, channels), BF16)
        xt[:, 0:LANES] = jnp.zeros((channels, LANES), BF16)

    widen(HALO - 16, 16)
    product_block(1)
    query_block(1)

    @pl.when(me < n_seq - 1)
    def _():
        halo[2].start()

    @pl.when(me > 0)
    def _():
        halo[1].wait_recv()

    st[md] = forward(0, split)
    send_stats(st, s_s, s_r)

    @pl.loop(0, blocks)
    def _(block):
        here = pl.ds(aligned(block, LANES), LANES)
        for ct in range(cts):
            inn[ct, here, :] = innt[ct * LANES : (ct + 1) * LANES, here].T

    def stack_blocks(g, carry):
        r = pl.ds(aligned(g, MEMBERS), MEMBERS)
        stack = [xt[r, b * LANES : (b + 1) * LANES].astype(F32) for b in range(blocks + 1)]
        stack.append(jnp.zeros((LANES - (blocks + 1) * MEMBERS, LANES), F32))
        xg[g] = jnp.concatenate(stack, axis=0).T.astype(BF16)
        return carry

    lax.fori_loop(0, groups, stack_blocks, 0, unroll=4)

    @pl.when(me > 0)
    def _():
        halo[2].wait_recv()

    widen(0, LANES)
    for ct in range(cts):
        for p in (1, 2):
            kv[(p - 1) * cts + ct, 0:LANES, :] = featured(p, ct, 0)

    token_scale = 1.0 / math.sqrt(rows * n_seq)

    def scales(slots, sends, receives, begin, end):
        @pl.loop(1, n_dp)
        def _(i):
            stat_copy(slots, sends, receives, i, lax.rem(md + i, n_dp)).wait_recv()

        whole = slots[0]
        for i in range(1, n_dp):
            whole = whole + slots[i]
        count = end - begin
        mean = whole * (1.0 / (channels * n_dp))
        rms = jnp.sqrt(mean[0:count] + 1e-05)
        scale_a = token_scale / rms
        scale_b = token_scale * mean[count : 2 * count] / (rms * rms * rms)
        lines_a = [scale_a[b : b + 1] for b in range(count)]
        lines_b = [scale_b[b : b + 1] for b in range(count)]
        for b in range(count):
            at[begin + b] = jnp.broadcast_to(lines_a[b], (LANES, LANES)).T
            bt[begin + b] = jnp.broadcast_to(lines_b[b], (LANES, LANES)).T
        return lines_a, lines_b

    def backward(lines_a, lines_b, begin, end, first):
        pad = jnp.zeros((MEMBERS, LANES), BF16)

        def padded(before, parts):
            after = LANES - before - len(parts) * MEMBERS
            return jnp.concatenate(
                [jnp.zeros((before, LANES), BF16)] * (before > 0) + parts + [jnp.zeros((after, LANES), BF16)],
                axis=0)

        def run(g, carry):
            r = pl.ds(aligned(g, MEMBERS), MEMBERS)
            parts = []
            for b in range(begin, end):
                cols = slice(b * LANES, (b + 1) * LANES)
                parts.append(
                    (ut[r, cols] * lines_a[b - begin] - wt[r, cols] * lines_b[b - begin]).astype(BF16))
            chain = [pad] + parts + [pad]
            left = jnp.concatenate(
                [jnp.concatenate(chain[b : b + 2], axis=1) for b in range(len(chain) - 1)], axis=0)
            grad = dot_nt(left, tob[g])
            for b in range(begin, end + 1):
                cols = slice(b * LANES, (b + 1) * LANES)
                piece = grad[(b - begin) * MEMBERS : (b - begin + 1) * MEMBERS]
                if b == end and not first:
                    piece = piece + pgt[r, cols]
                pgt[r, cols] = piece
            right = jnp.concatenate(
                [padded(begin * MEMBERS, parts), padded((begin + 1) * MEMBERS, parts)], axis=1)
            lagged = dot(xg[g], right)
            square = jnp.where(keep, lagged[:, LANES:], lagged[:, :LANES])
            total = square[0:8]
            for t in range(1, LANES // 8):
                total = total + pltpu.roll(square[8 * t : 8 * t + 8], LANES - 8 * t, 1)
            place = pl.ds(aligned(g, 8), 8)
            bases[place, :] = total if first else bases[place, :] + total
            return carry

        lax.fori_loop(0, groups, run, 0, unroll=8)

    def tail(ct, block, totals, inside):
        cols = slice(ct * LANES, (ct + 1) * LANES)
        gain = sk[ct : ct + 1, :].astype(F32)
        totals = list(totals)
        here = pl.ds(aligned(block, LANES), LANES)
        backed = pgt[cols, here].T
        windows = [
            pf.at[p * cts + ct, pl.ds(aligned(block, LANES), LANES + 16), :] for p in range(3)]
        step = 32

        def taps_of(part, begin, grad):
            for j in range(n_taps):
                term = grad * windows[part][16 - j + begin : 16 - j + begin + step, :]
                totals[part * 8 + j] = totals[part * 8 + j] + fold(term)

        for begin in range(0, LANES, step):
            local = pl.ds(pl.multiple_of(block * LANES + begin, 8), step)
            keys = kv[ct, local, :]
            values = kv[cts + ct, local, :]
            grad = backed[begin : begin + step]
            if inside:
                own = pl.ds(pl.multiple_of((block - 1) * LANES + begin, 16), step)
                queries = qv[ct, own, :]
                inner = inn[ct, own, :]
                first = at[block - 1, begin : begin + step, :]
                second = bt[block - 1, begin : begin + step, :]
                out_grad = cb[own, cols].astype(F32) * first - queries * inner * second
                conv = out_grad * queries
                grad = grad + gain * conv
                product = (keys * values).astype(BF16).astype(F32)
                totals[7] = totals[7] + fold(conv * product)
                taps_of(0, begin, out_grad * inner)
            taps_of(1, begin, grad * values)
            taps_of(2, begin, grad * keys)
        return tuple(totals)

    lines = scales(st2, t_s, t_r, split, blocks)
    backward(*lines, split, blocks, True)
    for ct in range(cts):
        totals = lax.fori_loop(
            split + 1, blocks + 1, lambda block, sums: tail(ct, block, sums, True), (zero8,) * 24)
        for n in range(24):
            tots[ct, n] = totals[n]

    lines = scales(st, s_s, s_r, 0, split)
    backward(*lines, 0, split, False)
    row_all = iota((8 * groups, LANES), 0)
    lag = bases[...]
    for k in (1, 2, 4):
        lag = jnp.where((row_all & k) != 0, pltpu.roll(lag, LANES - k, 1), lag)
    acc[48 : 48 + groups, :] = jnp.concatenate(
        [jnp.sum(lag[8 * g : 8 * g + 8], axis=0, keepdims=True) for g in range(groups)], axis=0)
    for ct in range(cts):
        totals = tail(ct, 0, [tots[ct, n] for n in range(24)], False)
        totals = lax.fori_loop(
            1, split + 1, lambda block, sums: tail(ct, block, sums, True), totals)
        for p in range(3):
            acc[(p * cts + ct) * 8 : (p * cts + ct) * 8 + 8, :] = jnp.concatenate(
                [jnp.sum(totals[p * 8 + j], axis=0, keepdims=True) for j in range(8)], axis=0)

    partner = {"seq": me + 1 - 2 * core}
    swap = pltpu.make_async_remote_copy(
        src_ref=acc.at[pl.ds(aligned(1 - core, half), half), :], dst_ref=slr,
        send_sem=a_s.at[0], recv_sem=a_r.at[0], device_id=partner, device_id_type=MESH)
    swap.start()

    def z_index(i):
        return lax.rem(mz + i, n_z)

    def exchange(slots, sends, receives, place, i, peer):
        return pltpu.make_async_remote_copy(
            src_ref=slots.at[place], dst_ref=slots.at[place], send_sem=sends.at[i],
            recv_sem=receives.at[place], device_id=peer(i), device_id_type=MESH)

    swap.wait_recv()
    sly[my] = (acc[pl.ds(aligned(core, half), half), :] + slr[...]).astype(BF16)

    for i in far_first(n_y, n_y, 1):
        exchange(sly, b_s, b_r, my, i, y_peer).start()

    @pl.loop(1, n_y)
    def _(i):
        exchange(sly, b_s, b_r, y_index(i), i, y_peer).wait_recv()

    part = sly[0].astype(F32)
    for i in range(1, n_y):
        part = part + sly[i].astype(F32)
    slz[mz] = part.astype(BF16)

    for i in far_first(n_z, n_z, 2):
        exchange(slz, c_s, c_r, mz, i, z_peer).start()

    @pl.loop(1, n_z)
    def _(i):
        exchange(slz, c_s, c_r, z_index(i), i, z_peer).wait_recv()

    for h in range(2):
        part = slz[h].astype(F32)
        for i in range(1, n_z // 2):
            part = part + slz[2 * i + h].astype(F32)
        out[h * half : (h + 1) * half, :] = part

    @pl.loop(1, n_dp)
    def _(i):
        stat_copy(st, s_s, s_r, i).wait_send()
        stat_copy(st2, t_s, t_r, i).wait_send()

    swap.wait_send()

    @pl.loop(1, n_y)
    def _(i):
        exchange(sly, b_s, b_r, my, i, y_peer).wait_send()

    @pl.loop(1, n_z)
    def _(i):
        exchange(slz, c_s, c_r, mz, i, z_peer).wait_send()

    @pl.when(me < n_seq - 1)
    def _():
        for copy in halo:
            copy.wait_send()


def unpack(packed, out_f, out_l, out_s):
    parts, n_taps, channels = out_f.shape
    cts = channels // LANES
    for ct in range(cts):
        cols = slice(ct * LANES, (ct + 1) * LANES)
        for p in range(parts):
            begin = (p * cts + ct) * 8
            out_f[p, :, cols] = packed[begin : begin + n_taps, :]
        out_s[:, cols] = packed[ct * 8 + 7 : ct * 8 + 8, :]
    out_l[...] = packed[parts * cts * 8 :, :]


def body(sizes, projected, featurizer, long_filter, skip_gain, out_cotangent):
    n_seq, n_dp = sizes
    parts, rows, channels = projected.shape
    n_taps = featurizer.shape[0]
    groups, filter_taps = long_filter.shape
    n_y = 1 << ((n_seq.bit_length() - 1) // 2)
    n_z = n_seq // n_y
    blocks = rows // LANES
    cts = channels // LANES
    geo = (n_seq, n_dp, n_y, n_z, rows, n_taps, channels)
    long = rows + LANES
    vmem = pltpu.VMEM
    dma = pltpu.SemaphoreType.DMA
    scratch = [
        vmem((3, HALO + rows, channels), BF16),
        vmem((rows, channels), BF16),
        vmem((3, n_taps, channels), BF16),
        vmem((groups, LANES), BF16),
        vmem((cts, LANES), BF16),
        vmem((groups, LANES), F32),
        vmem((3, 8, channels), F32),
        vmem((3 * cts, HALO + rows, LANES), F32),
        vmem((2 * cts, long, LANES), F32),
        vmem((cts, rows, LANES), F32),
        vmem((channels, long), BF16),
        vmem((channels, rows), F32),
        vmem((channels, rows), F32),
        vmem((channels, rows), F32),
        vmem((channels, rows), F32),
        vmem((channels, rows), F32),
        vmem((cts, rows, LANES), F32),
        vmem((groups, 2 * LANES, LANES), BF16),
        vmem((groups, LANES, 2 * LANES), BF16),
        vmem((groups, LANES, LANES), BF16),
        vmem((channels, long), F32),
        vmem((channels, LANES), F32),
        vmem((blocks, LANES, LANES), F32),
        vmem((blocks, LANES, LANES), F32),
        vmem((n_dp, blocks // 2 * 2, LANES), F32),
        vmem((n_dp, blocks // 2 * 2, LANES), F32),
        vmem((64, LANES), F32),
        vmem((cts, 24, 8, LANES), F32),
        vmem((8 * groups, LANES), F32),
        vmem((32, LANES), F32),
        vmem((n_y, 32, LANES), BF16),
        vmem((n_z, 32, LANES), BF16),
        dma((5,)), dma((3,)), dma((3,)),
        dma((n_dp,)), dma((n_dp,)),
        dma((n_dp,)), dma((n_dp,)),
        dma((1,)), dma((1,)),
        dma((n_y,)), dma((n_y,)),
        dma((n_z,)), dma((n_z,)),
    ]
    inside = pl.BlockSpec(memory_space=pltpu.VMEM)
    packed = pl.pallas_call(
        functools.partial(kernel, geo),
        out_shape=jax.ShapeDtypeStruct((64, LANES), F32),
        in_specs=[pl.BlockSpec(memory_space=pltpu.HBM)] * 5,
        out_specs=inside,
        scratch_shapes=scratch,
        compiler_params=pltpu.CompilerParams(
            collective_id=0, has_side_effects=True, vmem_limit_bytes=60 * 1024 * 1024),
    )(projected, featurizer.transpose(1, 0, 2), long_filter, skip_gain.reshape(cts, LANES), out_cotangent)
    feat, filt, skip = pl.pallas_call(
        unpack,
        out_shape=(
            jax.ShapeDtypeStruct((parts, n_taps, channels), F32),
            jax.ShapeDtypeStruct((groups, filter_taps), F32),
            jax.ShapeDtypeStruct((1, channels), F32),
        ),
        in_specs=[inside],
        out_specs=(inside,) * 3,
        compiler_params=pltpu.CompilerParams(vmem_limit_bytes=60 * 1024 * 1024),
    )(packed)
    return feat.transpose(1, 0, 2), filt, skip.reshape(channels)


def solution(mesh):
    sizes = (mesh.shape["seq"], mesh.shape["dp"])
    return jax.shard_map(
        functools.partial(body, sizes),
        mesh=mesh,
        in_specs=(
            P(None, "seq", "dp"),
            P(None, None, "dp"),
            P("dp", None),
            P("dp"),
            P("seq", "dp"),
        ),
        out_specs=(P(None, None, "dp"), P("dp", None), P("dp")),
        check_vma=False,
    )
```
